512 devices in a mesh: half: 4 (over x), row: 8 (over z), col: 16 (over y, core).
Axes of the slice: x: 4, y: 8, z: 8, core: 2. Of those that a mesh axis runs over, the one named last changes fastest.
Arguments:
- image_map: bfloat16 [4, 128, 256, 512], P('half', 'row', 'col'), may hold values from -15 to 15
- qkv_weight: bfloat16 [512, 1536], replicated, may hold values from -0.25 to 0.25
- proj_weight: bfloat16 [512, 512], replicated, may hold values from -0.25 to 0.25
- head_scale: float32 [16], replicated, may hold values from 2 to 20
- bias_table: float32 [16, 961], replicated, may hold values from -4 to 4
- attn_gain: float32 [512], replicated, may hold values from 0.25 to 1.75
- expert_ids: int32 [4, 128, 256, 1], P('half', 'row', 'col'), may hold values from 0 to 31
- gate_prob: float32 [4, 128, 256], P('half', 'row', 'col'), may hold values from 0.3 to 1
- w_in: bfloat16 [128, 512, 512], P(('row', 'col')), may hold values from -0.25 to 0.25
- w_out: bfloat16 [128, 512, 512], P(('row', 'col')), may hold values from -0.125 to 0.125
- expert_gain: float32 [512], replicated, may hold values from 0.25 to 1.75
- grad_out: bfloat16 [4, 128, 256, 512], P('half', 'row', 'col'), may hold values from -6 to 6
Outputs:
- block_out: bfloat16 [4, 128, 256, 512], P('half', 'row', 'col')
- grad_map: bfloat16 [4, 128, 256, 512], P('half', 'row', 'col')
- grad_w_in: float32 [128, 512, 512], P(('row', 'col'), 'half')
- grad_w_out: float32 [128, 512, 512], P(('row', 'col'), 'half')
The draws below stay inside these ranges and needn't reach their ends.
All inputs are finite; a program needn't handle non-finite values.
Results may differ from the reference program's by a relative error of at most 0.022.
Values may be sent and summed in bfloat16 or wider, within the bound.
No kernel may reach another device: no remote copies, remote signals or barrier semaphores. Data moves between devices by JAX's collectives and lax.ppermute only.
A program may use at most 192 MiB of HBM per device.

```python
import math
from functools import partial
import jax
import jax.numpy as jnp
from jax import lax

D = 512
HEADS = 16
FF = 2048
SPLIT = 4
EXPERTS = 32
WIN = 16
WROWS = 1
CAP = 8
IMGS = 4
MAP_H = 128
MAP_W = 256


def draw_image_map(key, part):
    key = jax.random.fold_in(key, 11)
    key_noise, key_scale = jax.random.split(key, 2)
    full_shape = (IMGS, MAP_H, MAP_W, D)
    scale_shape = (IMGS, MAP_H, MAP_W, 1)
    noise_part = jnp.clip(jax.random.normal(key_noise, full_shape, jnp.float32), -5.0, 5.0)
    row_scale = jnp.exp(jax.random.uniform(key_scale, scale_shape, jnp.float32, math.log(0.1), math.log(3.0)))
    return (noise_part * row_scale).astype(jnp.bfloat16)


def levels(stream_key, dims, cuts, smallest, largest):
    gain, own = 1.0, jax.random.fold_in(stream_key, 6)
    for position, shards_of in cuts:
        draws = jnp.exp(jax.random.uniform(jax.random.fold_in(own, position), (shards_of,), jnp.float32, smallest / len(cuts), largest / len(cuts)))
        gain = gain * jnp.repeat(draws, dims[position] // shards_of).reshape([-1 if axis == position else 1 for axis in range(len(dims))])
    return gain


def distinct(stream_key, rows, number_of, top, lift):
    ranking = jax.random.permutation(jax.random.fold_in(stream_key, 1), number_of)
    pull = ranking
    for power in range(3):
        pull = pull * pull // number_of
    pull = pull * lift // number_of
    lots = jax.random.randint(jax.random.fold_in(stream_key, 2), (rows, number_of), 0, 4096) + pull
    holders = jax.random.permutation(jax.random.fold_in(stream_key, 3), rows)[jnp.arange(number_of) % rows]
    lots = jnp.where(jnp.arange(rows)[:, None] == holders[None, :], 1 << 14, lots)
    merit = lots * number_of + jnp.arange(number_of)
    return lax.top_k(merit.astype(jnp.int32), top)[1].astype(jnp.int32)


def centred(key, dims, deviation, most, cuts=(), kind=jnp.bfloat16):
    level = levels(key, dims, cuts, -0.22, 0.18) if cuts else 1.0
    values = jax.random.normal(key, dims, jnp.float32) * deviation * level
    return jnp.minimum(jnp.maximum(values, -most), most).astype(kind)


def setup_inputs(seed: int = 0) -> dict:
    key_of = jax.random.split(jax.random.key(seed), 13)
    return {
        "image_map": draw_image_map(jax.random.fold_in(key_of[12], 71), 0),
        "qkv_weight": centred(key_of[1], (D, 3 * D), D ** -0.5, 0.25),
        "proj_weight": centred(key_of[2], (D, D), D ** -0.5, 0.25),
        "head_scale": jnp.clip(jnp.exp(jax.random.uniform(key_of[3], (HEADS,), jnp.float32, math.log(2.0), math.log(20.0))), 2.0, 20.0),
        "bias_table": centred(key_of[4], (HEADS, (2 * WIN - 1) * (2 * WIN - 1)), 1.0, 4.0, (), jnp.float32),
        "attn_gain": jnp.clip(1.0 + 0.15 * jax.random.normal(key_of[5], (D,), jnp.float32), 0.25, 1.75),
        "expert_ids": distinct(key_of[6], IMGS * MAP_H * MAP_W, EXPERTS, 1, 512).reshape((IMGS, MAP_H, MAP_W, 1)),
        "gate_prob": jnp.clip(0.3 + 0.7 * jax.random.uniform(key_of[7], (IMGS, MAP_H, MAP_W), jnp.float32) ** levels(key_of[7], (IMGS, MAP_H, MAP_W), ((0, 4), (1, 8), (2, 16)), -0.2, 0.2), 0.3, 1.0),
        "w_in": centred(key_of[8], (EXPERTS * SPLIT, D, FF // SPLIT), D ** -0.5, 0.25, ((0, 128),)),
        "w_out": centred(key_of[9], (EXPERTS * SPLIT, FF // SPLIT, D), FF ** -0.5, 0.125, ((0, 128),)),
        "expert_gain": jnp.clip(1.0 + 0.15 * jax.random.normal(key_of[10], (D,), jnp.float32), 0.25, 1.75),
        "grad_out": centred(key_of[11], (IMGS, MAP_H, MAP_W, D), 1.0, 6.0, ((0, 4), (1, 8), (2, 16))),
    }


EPS = 1e-05

def layer_norm(values_in, gain_vec):
    center = values_in - lax.optimization_barrier(jnp.mean(values_in, -1, keepdims=True))
    spread = lax.optimization_barrier(jnp.mean(center * center, -1, keepdims=True))
    return center * lax.rsqrt(spread + EPS) * gain_vec

def unit_rows(vectors):
    return vectors * lax.rsqrt(jnp.maximum(lax.optimization_barrier(jnp.sum(vectors * vectors, -1, keepdims=True)), 1.0))

def gelu_exact(hidden):
    return jax.nn.gelu(hidden, approximate=False)

def region_labels(row_pos, col_pos, map_height, map_width, window):
    shift_by = window // 2
    row_label = (row_pos >= map_height - window).astype(jnp.int32) + (row_pos >= map_height - shift_by).astype(jnp.int32)
    col_label = (col_pos >= map_width - window).astype(jnp.int32) + (col_pos >= map_width - shift_by).astype(jnp.int32)
    return row_label[:, None] * 3 + col_label[None, :]

def window_bias(bias_table, window):
    cell_pos = jnp.arange(window * window, dtype=jnp.int32)
    row_in = cell_pos // window
    col_in = cell_pos % window
    lookup = (row_in[:, None] - row_in[None, :] + window - 1) * (2 * window - 1) + col_in[:, None] - col_in[None, :] + window - 1
    return jnp.take(bias_table, lookup, axis=1)

def attend(windows, labels, qkv_weight, proj_weight, head_scale, pos_bias):
    win_count, cell_count, feat_width = windows.shape
    head_count = head_scale.shape[0]
    projected = jnp.dot(windows.reshape(win_count * cell_count, feat_width), qkv_weight, preferred_element_type=jnp.float32)
    projected = projected.reshape(win_count, cell_count, 3, head_count, feat_width // head_count)
    queries = unit_rows(projected[:, :, 0])
    key_unit = unit_rows(projected[:, :, 1])
    values = lax.optimization_barrier(projected[:, :, 2].astype(jnp.bfloat16)).astype(jnp.float32)
    scores = jnp.einsum('nqhd,nkhd->nhqk', queries, key_unit, precision=lax.Precision.HIGHEST) * head_scale[None, :, None, None] + pos_bias[None]
    scores = scores + jnp.where(labels[:, :, None] != labels[:, None, :], -100.0, 0.0)[:, None]
    weights = jnp.exp(scores)
    probabilities = lax.optimization_barrier((weights / lax.optimization_barrier(jnp.sum(weights, -1, keepdims=True))).astype(jnp.bfloat16)).astype(jnp.float32)
    heads_out = jnp.einsum('nhqk,nkhd->nqhd', probabilities, values, precision=lax.Precision.HIGHEST).astype(jnp.bfloat16)
    output = jnp.dot(heads_out.reshape(win_count * cell_count, feat_width), proj_weight, preferred_element_type=jnp.float32)
    return output.astype(jnp.bfloat16).reshape(win_count, cell_count, feat_width)

def windows_of(grid_field, window):
    img_count, map_height, map_width, depth_dim = grid_field.shape
    tiled_view = grid_field.reshape(img_count, map_height // window, window, map_width // window, window, depth_dim)
    return tiled_view.transpose(0, 1, 3, 2, 4, 5).reshape(-1, window * window, depth_dim)

def field_of(windows, img_count, map_height, map_width, window):
    depth_dim = windows.shape[-1]
    tiled_view = windows.reshape(img_count, map_height // window, map_width // window, window, window, depth_dim)
    return tiled_view.transpose(0, 1, 3, 2, 4, 5).reshape(img_count, map_height, map_width, depth_dim)

def to_blocks(grid_field, tile_height, tile_width):
    img_count, map_height, map_width = grid_field.shape[:3]
    rest_dims = grid_field.shape[3:]
    tiled_view = grid_field.reshape((img_count, map_height // tile_height, tile_height, map_width // tile_width, tile_width) + rest_dims)
    tiled_view = jnp.moveaxis(tiled_view, 3, 2)
    return tiled_view.reshape((img_count, map_height // tile_height, map_width // tile_width, tile_height * tile_width) + rest_dims)

def from_blocks(blocked, tile_height, tile_width):
    img_count, row_tiles, col_tiles = blocked.shape[:3]
    rest_dims = blocked.shape[4:]
    tiled_view = blocked.reshape((img_count, row_tiles, col_tiles, tile_height, tile_width) + rest_dims)
    tiled_view = jnp.moveaxis(tiled_view, 2, 3)
    return tiled_view.reshape((img_count, row_tiles * tile_height, col_tiles * tile_width) + rest_dims)

def reference(image_map, qkv_weight, proj_weight, head_scale, bias_table, attn_gain, expert_ids, gate_prob, w_in, w_out, expert_gain, grad_out):
    img_count, map_height, map_width, feat_width = image_map.shape
    shift_by = WIN // 2
    tile_height = WROWS * WIN
    cell_count = WIN * WIN
    pos_bias = window_bias(bias_table, WIN)
    labels = region_labels(jnp.arange(map_height, dtype=jnp.int32), jnp.arange(map_width, dtype=jnp.int32), map_height, map_width, WIN)
    label_win = windows_of(jnp.broadcast_to(labels[None, :, :, None], (img_count, map_height, map_width, 1)), WIN)[:, :, 0]
    win_total = label_win.shape[0]
    group_size = math.gcd(win_total, 8)
    group_count = win_total // group_size
    rolled = jnp.roll(image_map, (-shift_by, -shift_by), (1, 2))
    win_input = windows_of(rolled, WIN).reshape(group_count, group_size, cell_count, feat_width)
    label_groups = label_win.reshape(group_count, group_size, cell_count)

    def forward_group(operands):
        return attend(operands[0], operands[1], qkv_weight, proj_weight, head_scale, pos_bias)
    attn_win = lax.map(forward_group, (win_input, label_groups))
    attention = jnp.roll(field_of(attn_win.reshape(win_total, cell_count, feat_width), img_count, map_height, map_width, WIN), (shift_by, shift_by), (1, 2))
    normed, norm_vjp = jax.vjp(partial(layer_norm, gain_vec=attn_gain), attention.astype(jnp.float32))
    residual = image_map.astype(jnp.float32) + normed
    routed = to_blocks(residual.astype(jnp.bfloat16), tile_height, WIN)
    token_expert = to_blocks(expert_ids[..., 0], tile_height, WIN)
    onehot = (token_expert[..., None] == jnp.arange(EXPERTS, dtype=jnp.int32)).astype(jnp.int32)
    slot_index = lax.optimization_barrier(jnp.sum((jnp.cumsum(onehot, -2) - onehot) * onehot, -1))
    kept_mask = slot_index < CAP
    grid_shape = token_expert.shape
    image_index = jnp.broadcast_to(jnp.arange(grid_shape[0], dtype=jnp.int32)[:, None, None, None], grid_shape)
    row_index = jnp.broadcast_to(jnp.arange(grid_shape[1], dtype=jnp.int32)[None, :, None, None], grid_shape)
    col_index = jnp.broadcast_to(jnp.arange(grid_shape[2], dtype=jnp.int32)[None, None, :, None], grid_shape)
    buffer_shape = (EXPERTS, grid_shape[0], grid_shape[1], grid_shape[2], CAP, feat_width)
    slot_clip = jnp.minimum(slot_index, CAP - 1)

    def dispatch(token_rows):
        empty = jnp.zeros(buffer_shape, jnp.bfloat16)
        return empty.at[token_expert, image_index, row_index, col_index, slot_index].set(token_rows, mode='drop')

    def collect(buffers):
        picked = buffers[token_expert, image_index, row_index, col_index, slot_clip]
        return jnp.where(kept_mask[..., None], picked, 0.0)
    first_blocks = w_in.reshape(EXPERTS, SPLIT, feat_width, -1)
    second_blocks = w_out.reshape(EXPERTS, SPLIT, -1, feat_width)

    def expert_forward(operands):
        in_buffer, first_w, second_w = operands
        row_block = in_buffer.reshape(-1, feat_width)
        summed = jnp.zeros(row_block.shape, jnp.float32)
        for shard_id in range(SPLIT):
            hidden = jnp.dot(row_block, first_w[shard_id], preferred_element_type=jnp.float32)
            activated = gelu_exact(hidden).astype(jnp.bfloat16)
            shard_out = jnp.dot(activated, second_w[shard_id], preferred_element_type=jnp.float32).astype(jnp.bfloat16)
            summed = summed + lax.optimization_barrier(shard_out).astype(jnp.float32)
        return summed.reshape(in_buffer.shape)
    sent_rows = dispatch(routed)
    expert_out = collect(lax.map(expert_forward, (sent_rows, first_blocks, second_blocks)))
    gate_block = to_blocks(gate_prob, tile_height, WIN)

    def post_norm(values_in):
        return gate_block[..., None] * layer_norm(values_in, expert_gain)
    mixed_out, post_vjp = jax.vjp(post_norm, expert_out)
    residual_block = to_blocks(residual, tile_height, WIN)
    block_out = from_blocks(residual_block + mixed_out, tile_height, WIN).astype(jnp.bfloat16)
    grad_block = to_blocks(grad_out, tile_height, WIN).astype(jnp.float32)
    d_expert = post_vjp(grad_block)[0].astype(jnp.bfloat16)

    def expert_backward(operands):
        in_buffer, grad_buffer, first_w, second_w = operands
        row_block = in_buffer.reshape(-1, feat_width)
        grad_rows = grad_buffer.reshape(-1, feat_width)
        d_rows = jnp.zeros(row_block.shape, jnp.float32)
        first_list = []
        second_list = []
        for shard_id in range(SPLIT):
            hidden = jnp.dot(row_block, first_w[shard_id], preferred_element_type=jnp.float32)
            activated, gelu_vjp = jax.vjp(gelu_exact, hidden)
            activated = activated.astype(jnp.bfloat16)
            second_list.append(jnp.dot(activated.T, grad_rows, preferred_element_type=jnp.float32))
            d_active = jnp.dot(grad_rows, second_w[shard_id].T, preferred_element_type=jnp.float32)
            d_hidden = gelu_vjp(d_active)[0].astype(jnp.bfloat16)
            first_list.append(jnp.dot(row_block.T, d_hidden, preferred_element_type=jnp.float32))
            d_part = jnp.dot(d_hidden, first_w[shard_id].T, preferred_element_type=jnp.float32).astype(jnp.bfloat16)
            d_rows = d_rows + lax.optimization_barrier(d_part).astype(jnp.float32)
        return (d_rows.reshape(in_buffer.shape), jnp.stack(first_list), jnp.stack(second_list))
    d_buffers, first_grads, second_grads = lax.map(expert_backward, (sent_rows, dispatch(d_expert), first_blocks, second_blocks))
    grad_w_in = first_grads.reshape(w_in.shape)
    grad_w_out = second_grads.reshape(w_out.shape)
    d_resid = from_blocks(grad_block + collect(d_buffers), tile_height, WIN)
    d_attn = norm_vjp(d_resid)[0].astype(jnp.bfloat16)
    d_win = windows_of(jnp.roll(d_attn, (-shift_by, -shift_by), (1, 2)), WIN).reshape(group_count, group_size, cell_count, feat_width)

    def backward_group(operands):
        win_labels = operands[1]
        _, attend_vjp = jax.vjp(lambda win_values: attend(win_values, win_labels, qkv_weight, proj_weight, head_scale, pos_bias), operands[0])
        return attend_vjp(operands[2])[0]
    d_rolled_win = lax.map(backward_group, (win_input, label_groups, d_win))
    d_rolled = jnp.roll(field_of(d_rolled_win.reshape(win_total, cell_count, feat_width), img_count, map_height, map_width, WIN), (shift_by, shift_by), (1, 2))
    grad_map = (d_resid + d_rolled.astype(jnp.float32)).astype(jnp.bfloat16)
    return (block_out, grad_map, grad_w_in, grad_w_out)
```

```python
import jax
import jax.numpy as jnp
from jax import lax
from jax.experimental import pallas as pl
from jax.experimental.pallas import tpu as pltpu
from jax.sharding import PartitionSpec as P

SPLIT = 4
WIN = 16
HALF = WIN // 2
CELLS = WIN * WIN
HEAD_W = 32
EPS = 1e-05
TURNS = 2
BF16 = jnp.bfloat16
F32 = jnp.float32
VMEM_BYTES = 56 * 1024 * 1024


def dotg(a, b, ca, cb):
    return lax.dot_general(a, b, (((ca,), (cb,)), ((), ())), preferred_element_type=F32)


def call(body, outs, scratch=(), smem=0, total=0, gflop=1.0):
    in_specs = [pl.BlockSpec(memory_space=pltpu.SMEM)] * smem
    in_specs += [pl.BlockSpec(memory_space=pltpu.VMEM)] * (total - smem)
    return pl.pallas_call(
        body,
        out_shape=tuple(jax.ShapeDtypeStruct(s, d) for s, d in outs),
        in_specs=in_specs,
        out_specs=tuple(pl.BlockSpec(memory_space=pltpu.VMEM) for _ in outs),
        scratch_shapes=list(scratch),
        compiler_params=pltpu.CompilerParams(vmem_limit_bytes=VMEM_BYTES),
        cost_estimate=pl.CostEstimate(
            flops=int(gflop * 1e9), bytes_accessed=1 << 20, transcendentals=0
        ),
    )


def assemble(parts):
    a, b, c, d = (part.astype(F32) for part in parts)
    whole = jnp.concatenate([jnp.concatenate([a, b], 1), jnp.concatenate([c, d], 1)], 0)
    return whole.reshape(CELLS, whole.shape[-1])


def store_parts(whole, refs):
    tile = whole.reshape(WIN, WIN, whole.shape[-1])
    for i, ref in enumerate(refs):
        r, c = HALF * (i // 2), HALF * (i % 2)
        ref[...] = tile[r : r + HALF, c : c + HALF].astype(BF16)


def spread_table(table, low, high):
    heads, entries = table.shape
    lanes = 2 * CELLS
    padded = jnp.concatenate([table[...], jnp.zeros((heads, 2 * lanes - entries), F32)], 1)
    row = lax.broadcasted_iota(jnp.int32, (heads, lanes), 1) >> 4
    low_rows = jnp.zeros((heads, lanes), F32)
    high_rows = jnp.zeros((heads, lanes), F32)
    for j in range(2 * WIN - 1):
        left = (WIN - 1) * j
        first = pltpu.roll(padded, (2 * lanes - left) % (2 * lanes), 1)[:, :lanes]
        other = pltpu.roll(padded, 2 * lanes - left - WIN, 1)[:, :lanes]
        low_rows = jnp.where(row == j, first, low_rows)
        high_rows = jnp.where(row == j, other, high_rows)
    low[...] = low_rows
    high[...] = high_rows


def attention_forward(
    edge, scale, img, beside, below, corner, wqkv, proj, table,
    out0, out1, out2, out3, qs, ku, vt, weights, aux, ho, prj, strips, mask, low, high,
):
    heads = scale.shape[0]
    width = heads * HEAD_W
    own = img[...].astype(F32)[HALF:, HALF:]
    x = assemble((own, beside[...], below[...], corner[...])).astype(BF16)
    prj[...] = dotg(wqkv[...], x, 0, 1)
    spread_table(table, low, high)
    key = lax.broadcasted_iota(jnp.int32, (CELLS, CELLS), 0)
    qry = lax.broadcasted_iota(jnp.int32, (CELLS, CELLS), 1)
    row_diff = jnp.where((key >> 7) != (qry >> 7), edge[0], 0)
    col_diff = jnp.where(((key >> 3) & 1) != ((qry >> 3) & 1), edge[1], 0)
    mask[...] = jnp.where(row_diff + col_diff > 0, -100.0, 0.0)
    lanes = 2 * CELLS
    sub = lax.broadcasted_iota(jnp.int32, (WIN, lanes), 0)
    lane = lax.broadcasted_iota(jnp.int32, (WIN, lanes), 1)
    from_low = (lane & (WIN - 1)) <= sub

    def head(h, turn):
        at = pl.multiple_of(h * HEAD_W, HEAD_W)
        q = prj[pl.ds(at, HEAD_W), :]
        k = prj[pl.ds(width + at, HEAD_W), :]
        v = prj[pl.ds(2 * width + at, HEAD_W), :].astype(BF16)
        q_sq = jnp.sum(q * q, 0, keepdims=True)
        k_sq = jnp.sum(k * k, 0, keepdims=True)
        q = (q * (lax.rsqrt(jnp.maximum(q_sq, 1.0)) * scale[h])).astype(BF16)
        k = (k * lax.rsqrt(jnp.maximum(k_sq, 1.0))).astype(BF16)
        qs[pl.ds(at, HEAD_W), :] = q
        ku[pl.ds(at, HEAD_W), :] = k
        vt[pl.ds(at, HEAD_W), :] = v
        scores = dotg(k, q, 0, 0)
        low_rows = jnp.broadcast_to(low[pl.ds(h, 1), :], (WIN, lanes))
        high_rows = jnp.broadcast_to(high[pl.ds(h, 1), :], (WIN, lanes))
        strip = jnp.where(
            from_low,
            pltpu.roll(low_rows, lanes - WIN + 1, 1, stride=1, stride_axis=0),
            pltpu.roll(high_rows, 1, 1, stride=1, stride_axis=0),
        )
        strips[turn, 0] = strip
        for m in range(1, 8):
            strips[turn, m] = pltpu.roll(strip, lanes - WIN * m, 1)
        total = jnp.zeros((WIN, CELLS), F32)
        for a in range(WIN):
            far, m = divmod((WIN - 1 - a), 8)
            rows = slice(WIN * a, WIN * (a + 1))
            bias = strips[turn, m, :, 128 * far : 128 * far + CELLS]
            w = jnp.exp(scores[rows] + bias + mask[rows, :])
            total = total + w
            weights[h, rows, :] = w.astype(BF16)
        inv = 1.0 / jnp.sum(total, 0, keepdims=True)
        aux[h, 0:1, :] = inv
        aux[h, 1:2, :] = q_sq
        aux[h, 2:3, :] = k_sq
        ho[pl.ds(at, HEAD_W), :] = (dotg(v, weights[h], 1, 0) * inv).astype(BF16)

    def heads_of(i, carry):
        for turn in range(TURNS):
            head(i * TURNS + turn, turn)
        return carry

    lax.fori_loop(0, heads // TURNS, heads_of, 0)
    store_parts(dotg(ho[...], proj[...], 0, 0), (out0, out1, out2, out3))


def attention_backward(
    scale, d0, d1, d2, d3, wqkv, proj, qs, ku, vt, weights, aux, ho,
    out0, out1, out2, out3, dho, dprj,
):
    heads = scale.shape[0]
    width = heads * HEAD_W
    d_out = assemble((d0[...], d1[...], d2[...], d3[...])).astype(BF16)
    dho[...] = dotg(proj[...], d_out, 1, 1)

    def unit_grad(d_unit, unit, sq):
        inner = jnp.sum(d_unit * unit, 0, keepdims=True)
        share = jnp.where(sq > 1.0, 1.0, jnp.where(sq == 1.0, 0.5, 0.0))
        return (d_unit - unit * (inner * share)) * lax.rsqrt(jnp.maximum(sq, 1.0))

    def head(h):
        at = pl.multiple_of(h * HEAD_W, HEAD_W)
        here = pl.ds(at, HEAD_W)
        q, k, v = qs[here, :], ku[here, :], vt[here, :]
        inv = aux[h, 0:1, :]
        d_ho = dho[here, :].astype(BF16).astype(F32)
        delta = jnp.sum(d_ho * ho[here, :].astype(F32), 0, keepdims=True) * inv
        d_ho = (d_ho * inv).astype(BF16)
        w = weights[h]
        d_w = dotg(v, d_ho, 0, 0)
        d_s = (w.astype(F32) * (d_w - delta)).astype(BF16)
        d_q = dotg(k, d_s, 1, 0) * scale[h]
        d_k = dotg(q, d_s, 1, 1)
        d_v = dotg(d_ho, w, 1, 1)
        q_unit = q.astype(F32) * (1.0 / scale[h])
        dprj[here, :] = unit_grad(d_q, q_unit, aux[h, 1:2, :]).astype(BF16)
        dprj[pl.ds(width + at, HEAD_W), :] = unit_grad(d_k, k.astype(F32), aux[h, 2:3, :]).astype(BF16)
        dprj[pl.ds(2 * width + at, HEAD_W), :] = d_v.astype(BF16)

    def heads_of(i, carry):
        for turn in range(TURNS):
            head(i * TURNS + turn)
        return carry

    lax.fori_loop(0, heads // TURNS, heads_of, 0)
    store_parts(dotg(dprj[...], wqkv[...], 0, 1), (out0, out1, out2, out3))


def normal(values):
    center = values - jnp.mean(values, -1, keepdims=True)
    rstd = lax.rsqrt(jnp.mean(center * center, -1, keepdims=True) + EPS)
    return center * rstd, rstd


def norm_grad(unit, rstd, d_unit):
    return rstd * (
        d_unit
        - jnp.mean(d_unit, -1, keepdims=True)
        - unit * jnp.mean(d_unit * unit, -1, keepdims=True)
    )


def column(field):
    row = lax.broadcasted_iota(jnp.int32, (CELLS, WIN), 0)
    col = lax.broadcasted_iota(jnp.int32, (CELLS, WIN), 1)
    pick = jnp.where((row >> 4) == col, 1.0, 0.0)
    rows = lax.dot_general(
        pick, field, (((1,), (0,)), ((), ())),
        preferred_element_type=F32, precision=lax.Precision.HIGHEST,
    )
    return jnp.sum(jnp.where((row & (WIN - 1)) == col, rows, 0.0), 1, keepdims=True)


def place_tokens(ids, gate, grad, place, packed, experts, cap):
    expert = column(ids[...].astype(F32)).astype(jnp.int32)
    matches = expert == lax.broadcasted_iota(jnp.int32, (CELLS, experts), 1)
    later = lax.broadcasted_iota(jnp.int32, (CELLS, CELLS), 0)
    sooner = lax.broadcasted_iota(jnp.int32, (CELLS, CELLS), 1)
    earlier = jnp.where(later > sooner, 1.0, 0.0).astype(BF16)
    before = dotg(earlier, jnp.where(matches, 1.0, 0.0).astype(BF16), 1, 0)
    slot = jnp.sum(jnp.where(matches, before, 0.0), 1, keepdims=True).astype(jnp.int32)
    target = jnp.where(slot < cap, expert * cap + slot, -1)
    slots = lax.broadcasted_iota(jnp.int32, (CELLS, experts * cap), 1)
    where_to = jnp.where(target == slots, 1.0, 0.0).astype(BF16)
    place[...] = where_to
    weighted = (grad[...].astype(F32) * column(gate[...])).astype(BF16)
    packed[...] = dotg(where_to, weighted, 0, 0).astype(BF16).reshape(packed.shape)


def pack_residual(att0, att1, att2, att3, img, gain, place, packed, att):
    attention = assemble((att0[...], att1[...], att2[...], att3[...]))
    att[...] = attention.astype(BF16)
    unit, _ = normal(attention)
    routed = (img[...].astype(F32) + unit * gain[...]).astype(BF16)
    packed[...] = dotg(place[...], routed, 0, 0).astype(BF16).reshape(packed.shape)


def residual_grad(att, gain, place, grad, back, d_resid, d0, d1, d2, d3):
    unit, rstd = normal(att[...].astype(F32))
    total = grad[...].astype(F32) + dotg(place[...], back[...].reshape(grad.shape), 1, 0)
    d_resid[...] = total
    store_parts(norm_grad(unit, rstd, total * gain[...]), (d0, d1, d2, d3))


def finish_block(att, img, gain, place, gate, mixed, out):
    unit, _ = normal(att[...].astype(F32))
    residual = img[...].astype(F32) + unit * gain[...]
    added = column(gate[...]) * dotg(place[...], mixed[...].reshape(img.shape), 1, 0)
    out[...] = (residual + added).astype(BF16)


def gelu_parts(hidden):
    cdf = 0.5 * (1.0 + lax.erf(hidden * 0.7071067811865476))
    pdf = jnp.exp(hidden * hidden * -0.5) * 0.3989422804014327
    return hidden * cdf, cdf + hidden * pdf


def expert_rows(rows, grad, gain, near, far, mixed, d_expert, d_rows, slope):
    half = near.shape[1] // 2
    flat = d_expert.shape
    here = rows[...].reshape(flat)
    blocks = [(ref, i) for ref in (near, far) for i in range(2)]
    total = jnp.zeros(flat, F32)
    for s, (ref, i) in enumerate(blocks):
        act, slope[s] = gelu_parts(dotg(here, ref[i, :half, :], 1, 0))
        total = total + dotg(act.astype(BF16), ref[i, half:, :], 1, 0).astype(BF16).astype(F32)
    unit, rstd = normal(total)
    mixed[...] = (unit * gain[...]).astype(BF16).reshape(mixed.shape)
    d_out = norm_grad(unit, rstd, grad[...].reshape(flat).astype(F32) * gain[...]).astype(BF16)
    d_expert[...] = d_out
    total = jnp.zeros(flat, F32)
    for s, (ref, i) in enumerate(blocks):
        d_hidden = (dotg(d_out, ref[i, half:, :], 1, 1) * slope[s]).astype(BF16)
        total = total + dotg(d_hidden, ref[i, :half, :], 1, 1).astype(BF16).astype(F32)
    d_rows[...] = total.astype(BF16).reshape(d_rows.shape)


def expert_grads(place, rows, grad0, grad1, grad2, grad3, w_in, w_out, both):
    count, width = grad0.shape
    d_in = jnp.zeros(w_in.shape, F32)
    d_out = jnp.zeros(w_out.shape, F32)
    for s, grad in enumerate((grad0, grad1, grad2, grad3)):
        part = rows[pl.ds(pl.multiple_of((place[0] ^ s) * count, count), count), :]
        act, slope = gelu_parts(dotg(part, w_in[...], 1, 0))
        d_out = d_out + dotg(act.astype(BF16), grad[...], 0, 0)
        d_hidden = (dotg(grad[...], w_out[...], 1, 1) * slope).astype(BF16)
        d_in = d_in + dotg(part, d_hidden, 0, 0)
    both[:, : w_in.shape[1]] = d_in.astype(BF16)
    both[:, w_in.shape[1] :] = d_out.astype(BF16)


def send(piece, down, right):
    rows, cols = lax.axis_size("row"), lax.axis_size("col")
    if right == 0:
        return lax.ppermute(piece, "row", [(i, (i + down) % rows) for i in range(rows)])
    if down == 0:
        return lax.ppermute(piece, "col", [(i, (i + right) % cols) for i in range(cols)])
    route = [
        (r * cols + c, (r + down) % rows * cols + (c + right) % cols)
        for r in range(rows)
        for c in range(cols)
    ]
    return lax.ppermute(piece, ("row", "col"), route)


def to_window(part0, part1, part2, part3):
    return part3, send(part2, 0, -1), send(part1, -1, 0), send(part0, -1, -1)


def from_window(part0, part1, part2, part3):
    return send(part3, 1, 1), send(part2, 1, 0), send(part1, 0, 1), part0


def exchange(parts):
    return lax.all_to_all(parts, ("row", "col"), split_axis=0, concat_axis=0, tiled=True)


def group_gather(rows):
    cols = lax.axis_size("col")
    groups = [[g + i for i in range(SPLIT)] for g in range(0, cols, SPLIT)]
    return lax.all_gather(rows, "col", axis_index_groups=groups, axis=0, tiled=True)


def swap(piece, bit):
    return lax.ppermute(piece, "col", [(i, i ^ bit) for i in range(lax.axis_size("col"))])


def gather_blocks(blocks):
    cols = lax.axis_size("col")
    groups = [[g + i, g + i + 2] for g in range(0, cols, SPLIT) for i in range(2)]
    return lax.all_gather(blocks, "col", axis_index_groups=groups, axis=0, tiled=False)


def shards(
    image_map,
    qkv_weight,
    proj_weight,
    head_scale,
    bias_table,
    attn_gain,
    expert_ids,
    gate_prob,
    w_in,
    w_out,
    expert_gain,
    grad_out,
):
    width = image_map.shape[3]
    heads = head_scale.shape[0]
    row_count, col_count = lax.axis_size("row"), lax.axis_size("col")
    devices = row_count * col_count
    experts = devices // SPLIT
    cap = CELLS // experts
    slots = experts * cap
    tile = (WIN, WIN, width)
    quarter = (HALF, HALF, width)
    flat = (CELLS, width)
    parts = (devices, slots // devices, width)
    tile_img = image_map[0]
    img = tile_img.reshape(flat)
    grad = grad_out[0].reshape(flat)
    ids = expert_ids.reshape(WIN, WIN)
    gate = gate_prob.reshape(WIN, WIN)
    a_gain = attn_gain.reshape(1, width)
    e_gain = expert_gain.reshape(1, width)

    pieces = (tile_img[:HALF, :HALF], tile_img[:HALF, HALF:], tile_img[HALF:, :HALF])
    _, beside, below, corner = to_window(*pieces, None)
    place, grad_packed = call(
        lambda *refs: place_tokens(*refs, experts=experts, cap=cap),
        [((CELLS, slots), BF16), (parts, BF16)],
        total=3,
    )(ids, gate, grad)
    grad_slots = exchange(grad_packed)
    first_w, second_w, _ = lax.optimization_barrier((w_in[0], w_out[0], pieces))
    near = gather_blocks(jnp.concatenate([first_w, second_w], 0))
    edge = jnp.stack(
        [lax.axis_index("row") == row_count - 1, lax.axis_index("col") == col_count - 1]
    ).astype(jnp.int32)
    corner, _ = lax.optimization_barrier((corner, grad_packed))
    *attn_parts, qs, ku, vt, weights, aux, ho = call(
        attention_forward,
        [(quarter, BF16)] * 4
        + [((width, CELLS), BF16)] * 3
        + [
            ((heads, CELLS, CELLS), BF16),
            ((heads, 8, CELLS), F32),
            ((width, CELLS), BF16),
        ],
        [
            pltpu.VMEM((3 * width, CELLS), F32),
            pltpu.VMEM((TURNS, 8, WIN, 2 * CELLS), F32),
            pltpu.VMEM((CELLS, CELLS), F32),
            pltpu.VMEM((heads, 2 * CELLS), F32),
            pltpu.VMEM((heads, 2 * CELLS), F32),
        ],
        smem=2,
        total=9,
        gflop=8.0,
    )(edge, head_scale, tile_img, beside, below, corner, qkv_weight, proj_weight, bias_table)
    att_parts = from_window(*attn_parts)
    *att_parts, grad_slots = lax.optimization_barrier((*att_parts, grad_slots))
    packed, att = call(pack_residual, [(parts, BF16), (flat, BF16)], total=7)(
        *att_parts, img, a_gain, place
    )
    near, _ = lax.optimization_barrier((near, packed))
    far = swap(near, 1)
    rows = exchange(packed)
    all_rows = group_gather(rows.reshape(flat))
    mixed, d_expert, d_rows = call(
        expert_rows,
        [(parts, BF16), (flat, BF16), (parts, BF16)],
        [pltpu.VMEM((SPLIT,) + flat, F32)],
        total=5,
        gflop=2.0,
    )(rows, grad_slots, e_gain, near, far)
    back = exchange(d_rows)
    across = swap(d_expert, 2)
    grads = (d_expert, swap(d_expert, 1), across, swap(across, 1))
    place_in_group = (lax.axis_index("col") % SPLIT).astype(jnp.int32).reshape(1)
    (both,) = call(
        expert_grads, [((w_in.shape[1], 2 * w_in.shape[2]), BF16)], smem=1, total=8, gflop=0.01
    )(place_in_group, all_rows, *grads, w_in[0], w_out[0])
    back, both = lax.optimization_barrier((back, both))
    both = lax.psum_scatter(both, "half", scatter_dimension=0, tiled=True).astype(F32)
    grad_w_in, grad_w_out = both[None, :, : w_in.shape[2]], both[None, :, w_in.shape[2] :]
    d_resid, *d_att = call(residual_grad, [(flat, F32)] + [(quarter, BF16)] * 4, total=5)(
        att, a_gain, place, grad, back
    )
    mixed, *d_att = lax.optimization_barrier((mixed, *d_att))
    mixed_back = exchange(mixed)
    d_rolled = call(
        attention_backward,
        [(quarter, BF16)] * 4,
        [pltpu.VMEM((width, CELLS), F32), pltpu.VMEM((3 * width, CELLS), BF16)],
        smem=1,
        total=13,
        gflop=8.0,
    )(head_scale, *to_window(*d_att), qkv_weight, proj_weight, qs, ku, vt, weights, aux, ho)
    *d_rolled, mixed_back = lax.optimization_barrier((*d_rolled, mixed_back))
    (block_out,) = call(finish_block, [(flat, BF16)], total=6)(
        att, img, a_gain, place, gate, mixed_back
    )
    top_left, top_right, bottom_left, bottom_right = from_window(*d_rolled)
    returned = jnp.concatenate(
        [
            jnp.concatenate([top_left, top_right], 1),
            jnp.concatenate([bottom_left, bottom_right], 1),
        ],
        0,
    )
    grad_map = (d_resid.reshape(tile) + returned.astype(F32)).astype(BF16)
    return (block_out.reshape(image_map.shape), grad_map[None], grad_w_in, grad_w_out)


def solution(mesh):
    tokens = P("half", "row", "col", None)
    in_specs = (
        tokens,
        P(),
        P(),
        P(),
        P(),
        P(),
        tokens,
        P("half", "row", "col"),
        P(("row", "col"), None, None),
        P(("row", "col"), None, None),
        P(),
        tokens,
    )
    out_specs = (
        tokens,
        tokens,
        P(("row", "col"), "half", None),
        P(("row", "col"), "half", None),
    )
    return jax.shard_map(shards, mesh=mesh, in_specs=in_specs, out_specs=out_specs, check_vma=False)
```

```python
import jax
import jax.numpy as jnp
from jax import lax
from jax.experimental import pallas as pl
from jax.experimental.pallas import tpu as pltpu
from jax.sharding import PartitionSpec as P

SPLIT = 4
WIN = 16
HALF = WIN // 2
CELLS = WIN * WIN
HEAD_W = 32
EPS = 1e-05
TURNS = 8
BF16 = jnp.bfloat16
F32 = jnp.float32
VMEM_BYTES = 24 * 1024 * 1024


def dotg(a, b, ca, cb):
    return lax.dot_general(a, b, (((ca,), (cb,)), ((), ())), preferred_element_type=F32)


def in_vmem(*arrays):
    return [pltpu.with_memory_space_constraint(a, pltpu.VMEM) for a in arrays]


def call(body, outs, scratch=(), smem=0, total=0, gflop=1.0):
    in_specs = [pl.BlockSpec(memory_space=pltpu.SMEM)] * smem
    in_specs += [pl.BlockSpec(memory_space=pltpu.VMEM)] * (total - smem)
    return pl.pallas_call(
        body,
        out_shape=tuple(jax.ShapeDtypeStruct(s, d) for s, d in outs),
        in_specs=in_specs,
        out_specs=tuple(pl.BlockSpec(memory_space=pltpu.VMEM) for _ in outs),
        scratch_shapes=list(scratch),
        compiler_params=pltpu.CompilerParams(vmem_limit_bytes=VMEM_BYTES),
        cost_estimate=pl.CostEstimate(
            flops=int(gflop * 1e9), bytes_accessed=1 << 20, transcendentals=0
        ),
    )


def assemble(parts):
    a, b, c, d = (part.astype(F32) for part in parts)
    whole = jnp.concatenate([jnp.concatenate([a, b], 1), jnp.concatenate([c, d], 1)], 0)
    return whole.reshape(CELLS, whole.shape[-1])


def store_parts(whole, refs):
    tile = whole.reshape(WIN, WIN, whole.shape[-1])
    for i, ref in enumerate(refs):
        r, c = HALF * (i // 2), HALF * (i % 2)
        ref[...] = tile[r : r + HALF, c : c + HALF].astype(BF16)


def spread_table(table, low, high):
    heads, entries = table.shape
    lanes = 2 * CELLS
    padded = jnp.concatenate([table[...], jnp.zeros((heads, 2 * lanes - entries), F32)], 1)
    row = lax.broadcasted_iota(jnp.int32, (heads, lanes), 1) >> 4
    low_rows = jnp.zeros((heads, lanes), F32)
    high_rows = jnp.zeros((heads, lanes), F32)
    for j in range(2 * WIN - 1):
        left = (WIN - 1) * j
        first = pltpu.roll(padded, (2 * lanes - left) % (2 * lanes), 1)[:, :lanes]
        other = pltpu.roll(padded, 2 * lanes - left - WIN, 1)[:, :lanes]
        low_rows = jnp.where(row == j, first, low_rows)
        high_rows = jnp.where(row == j, other, high_rows)
    low[...] = low_rows
    high[...] = high_rows


def attention_forward(
    edge, scale, img, beside, below, corner, wqkv, proj, table,
    out0, out1, out2, out3, qs, ku, vt, weights, aux, ho, prj, strips, mask, low, high,
):
    heads = scale.shape[0]
    width = heads * HEAD_W
    own = img[...].astype(F32)[HALF:, HALF:]
    x = assemble((own, beside[...], below[...], corner[...])).astype(BF16)
    prj[...] = dotg(wqkv[...], x, 0, 1)
    spread_table(table, low, high)
    key = lax.broadcasted_iota(jnp.int32, (CELLS, CELLS), 0)
    qry = lax.broadcasted_iota(jnp.int32, (CELLS, CELLS), 1)
    row_diff = jnp.where((key >> 7) != (qry >> 7), edge[0], 0)
    col_diff = jnp.where(((key >> 3) & 1) != ((qry >> 3) & 1), edge[1], 0)
    mask[...] = jnp.where(row_diff + col_diff > 0, -100.0, 0.0)
    lanes = 2 * CELLS
    sub = lax.broadcasted_iota(jnp.int32, (WIN, lanes), 0)
    lane = lax.broadcasted_iota(jnp.int32, (WIN, lanes), 1)
    from_low = (lane & (WIN - 1)) <= sub

    def head(h, turn):
        at = pl.multiple_of(h * HEAD_W, HEAD_W)
        q = prj[pl.ds(at, HEAD_W), :]
        k = prj[pl.ds(width + at, HEAD_W), :]
        v = prj[pl.ds(2 * width + at, HEAD_W), :].astype(BF16)
        q_sq = jnp.sum(q * q, 0, keepdims=True)
        k_sq = jnp.sum(k * k, 0, keepdims=True)
        q = (q * (lax.rsqrt(jnp.maximum(q_sq, 1.0)) * scale[h])).astype(BF16)
        k = (k * lax.rsqrt(jnp.maximum(k_sq, 1.0))).astype(BF16)
        qs[pl.ds(at, HEAD_W), :] = q
        ku[pl.ds(at, HEAD_W), :] = k
        vt[pl.ds(at, HEAD_W), :] = v
        scores = dotg(k, q, 0, 0)
        low_rows = jnp.broadcast_to(low[pl.ds(h, 1), :], (WIN, lanes))
        high_rows = jnp.broadcast_to(high[pl.ds(h, 1), :], (WIN, lanes))
        strip = jnp.where(
            from_low,
            pltpu.roll(low_rows, lanes - WIN + 1, 1, stride=1, stride_axis=0),
            pltpu.roll(high_rows, 1, 1, stride=1, stride_axis=0),
        )
        strips[turn, 0] = strip
        for m in range(1, 8):
            strips[turn, m] = pltpu.roll(strip, lanes - WIN * m, 1)
        total = jnp.zeros((WIN, CELLS), F32)
        for a in range(WIN):
            far, m = divmod((WIN - 1 - a), 8)
            rows = slice(WIN * a, WIN * (a + 1))
            bias = strips[turn, m, :, 128 * far : 128 * far + CELLS]
            w = jnp.exp(scores[rows] + bias + mask[rows, :])
            total = total + w
            weights[h, rows, :] = w.astype(BF16)
        inv = 1.0 / jnp.sum(total, 0, keepdims=True)
        aux[h, 0:1, :] = inv
        aux[h, 1:2, :] = q_sq
        aux[h, 2:3, :] = k_sq
        ho[pl.ds(at, HEAD_W), :] = (dotg(v, weights[h], 1, 0) * inv).astype(BF16)

    def heads_of(i, carry):
        for turn in range(TURNS):
            head(i * TURNS + turn, turn)
        return carry

    lax.fori_loop(0, heads // TURNS, heads_of, 0)
    store_parts(dotg(ho[...], proj[...], 0, 0), (out0, out1, out2, out3))


def attention_backward(
    scale, d0, d1, d2, d3, wqkv, proj, qs, ku, vt, weights, aux, ho,
    out0, out1, out2, out3, dho, dprj,
):
    heads = scale.shape[0]
    width = heads * HEAD_W
    d_out = assemble((d0[...], d1[...], d2[...], d3[...])).astype(BF16)
    dho[...] = dotg(proj[...], d_out, 1, 1)

    def unit_grad(d_unit, unit, sq):
        inner = jnp.sum(d_unit * unit, 0, keepdims=True)
        share = jnp.where(sq > 1.0, 1.0, jnp.where(sq == 1.0, 0.5, 0.0))
        return (d_unit - unit * (inner * share)) * lax.rsqrt(jnp.maximum(sq, 1.0))

    def head(h):
        at = pl.multiple_of(h * HEAD_W, HEAD_W)
        here = pl.ds(at, HEAD_W)
        q, k, v = qs[here, :], ku[here, :], vt[here, :]
        inv = aux[h, 0:1, :]
        d_ho = dho[here, :].astype(BF16).astype(F32)
        delta = jnp.sum(d_ho * ho[here, :].astype(F32), 0, keepdims=True) * inv
        d_ho = (d_ho * inv).astype(BF16)
        w = weights[h]
        d_w = dotg(v, d_ho, 0, 0)
        d_s = (w.astype(F32) * (d_w - delta)).astype(BF16)
        d_q = dotg(k, d_s, 1, 0) * scale[h]
        d_k = dotg(q, d_s, 1, 1)
        d_v = dotg(d_ho, w, 1, 1)
        q_unit = q.astype(F32) * (1.0 / scale[h])
        dprj[here, :] = unit_grad(d_q, q_unit, aux[h, 1:2, :]).astype(BF16)
        dprj[pl.ds(width + at, HEAD_W), :] = unit_grad(d_k, k.astype(F32), aux[h, 2:3, :]).astype(BF16)
        dprj[pl.ds(2 * width + at, HEAD_W), :] = d_v.astype(BF16)

    def heads_of(i, carry):
        for turn in range(TURNS):
            head(i * TURNS + turn)
        return carry

    lax.fori_loop(0, heads // TURNS, heads_of, 0)
    store_parts(dotg(dprj[...], wqkv[...], 0, 1), (out0, out1, out2, out3))


def normal(values):
    center = values - jnp.mean(values, -1, keepdims=True)
    rstd = lax.rsqrt(jnp.mean(center * center, -1, keepdims=True) + EPS)
    return center * rstd, rstd


def norm_grad(unit, rstd, d_unit):
    return rstd * (
        d_unit
        - jnp.mean(d_unit, -1, keepdims=True)
        - unit * jnp.mean(d_unit * unit, -1, keepdims=True)
    )


def column(field):
    row = lax.broadcasted_iota(jnp.int32, (CELLS, WIN), 0)
    col = lax.broadcasted_iota(jnp.int32, (CELLS, WIN), 1)
    pick = jnp.where((row >> 4) == col, 1.0, 0.0)
    rows = lax.dot_general(
        pick, field, (((1,), (0,)), ((), ())),
        preferred_element_type=F32, precision=lax.Precision.HIGHEST,
    )
    return jnp.sum(jnp.where((row & (WIN - 1)) == col, rows, 0.0), 1, keepdims=True)


def both_in(out, first, second):
    shape = (out.shape[0], out.shape[1] // 2, out.shape[2])
    out[...] = jnp.concatenate([first.reshape(shape), second.reshape(shape)], 1)


def one_of(both, which):
    count = both.shape[1] // 2
    part = both[:, which * count : (which + 1) * count, :]
    return part.reshape(part.shape[0] * count, part.shape[2])


def place_tokens(ids, gate, grad, place, packed, experts, cap):
    expert = column(ids[...].astype(F32)).astype(jnp.int32)
    matches = expert == lax.broadcasted_iota(jnp.int32, (CELLS, experts), 1)
    later = lax.broadcasted_iota(jnp.int32, (CELLS, CELLS), 0)
    sooner = lax.broadcasted_iota(jnp.int32, (CELLS, CELLS), 1)
    earlier = jnp.where(later > sooner, 1.0, 0.0).astype(BF16)
    before = dotg(earlier, jnp.where(matches, 1.0, 0.0).astype(BF16), 1, 0)
    slot = jnp.sum(jnp.where(matches, before, 0.0), 1, keepdims=True).astype(jnp.int32)
    target = jnp.where(slot < cap, expert * cap + slot, -1)
    slots = lax.broadcasted_iota(jnp.int32, (CELLS, experts * cap), 1)
    where_to = jnp.where(target == slots, 1.0, 0.0).astype(BF16)
    place[...] = where_to
    weighted = (grad[...].astype(F32) * column(gate[...])).astype(BF16)
    packed[...] = dotg(where_to, weighted, 0, 0).astype(BF16)


def pack_residual(att0, att1, att2, att3, img, gain, place, grad_packed, packed, att):
    attention = assemble((att0[...], att1[...], att2[...], att3[...]))
    att[...] = attention.astype(BF16)
    unit, _ = normal(attention)
    routed = (img[...].astype(F32) + unit * gain[...]).astype(BF16)
    both_in(packed, dotg(place[...], routed, 0, 0).astype(BF16), grad_packed[...])


def residual_grad(att, gain, place, grad, back, d_resid, d0, d1, d2, d3):
    unit, rstd = normal(att[...].astype(F32))
    total = grad[...].astype(F32) + dotg(place[...], one_of(back[...], 0), 1, 0)
    d_resid[...] = total
    store_parts(norm_grad(unit, rstd, total * gain[...]), (d0, d1, d2, d3))


def finish_block(att, img, gain, place, gate, back, out):
    unit, _ = normal(att[...].astype(F32))
    residual = img[...].astype(F32) + unit * gain[...]
    added = column(gate[...]) * dotg(place[...], one_of(back[...], 1), 1, 0)
    out[...] = (residual + added).astype(BF16)


def gelu_parts(hidden):
    cdf = 0.5 * (1.0 + lax.erf(hidden * 0.7071067811865476))
    pdf = jnp.exp(hidden * hidden * -0.5) * 0.3989422804014327
    return hidden * cdf, cdf + hidden * pdf


def expert_hidden(sent, block0, block1, block2, block3, rows, act, slope):
    here = one_of(sent[...], 0)
    rows[...] = here
    for s, ref in enumerate((block0, block1, block2, block3)):
        value, grad = gelu_parts(dotg(here, ref[...], 1, 0))
        act[s] = value.astype(BF16)
        slope[s] = grad.astype(BF16)


def expert_rows(sent, gain, act, slope, *refs):
    w_in, w_out = refs[0:2] + refs[4:6], refs[2:4] + refs[6:8]
    d_expert, back = refs[8:]
    flat = d_expert.shape
    grad = one_of(sent[...], 1)
    total = jnp.zeros(flat, F32)
    for s, v in enumerate(w_out):
        total = total + dotg(act[s], v[...], 1, 0).astype(BF16).astype(F32)
    unit, rstd = normal(total)
    mixed = (unit * gain[...]).astype(BF16)
    d_out = norm_grad(unit, rstd, grad.astype(F32) * gain[...]).astype(BF16)
    d_expert[...] = d_out
    total = jnp.zeros(flat, F32)
    for s, (w, v) in enumerate(zip(w_in, w_out, strict=True)):
        d_hidden = (dotg(d_out, v[...], 1, 1) * slope[s].astype(F32)).astype(BF16)
        total = total + dotg(d_hidden, w[...], 1, 1).astype(BF16).astype(F32)
    both_in(back, total.astype(BF16), mixed)


def expert_grads(*refs):
    rows, grads, (w_in, w_out, both) = refs[:SPLIT], refs[SPLIT : 2 * SPLIT], refs[2 * SPLIT :]
    d_in = jnp.zeros(w_in.shape, F32)
    d_out = jnp.zeros(w_out.shape, F32)
    for part, grad in zip(rows, grads, strict=True):
        part = part[...]
        act, slope = gelu_parts(dotg(part, w_in[...], 1, 0))
        d_out = d_out + dotg(act.astype(BF16), grad[...], 0, 0)
        d_hidden = (dotg(grad[...], w_out[...], 1, 1) * slope).astype(BF16)
        d_in = d_in + dotg(part, d_hidden, 0, 0)
    both[:, : w_in.shape[1]] = d_in.astype(BF16)
    both[:, w_in.shape[1] :] = d_out.astype(BF16)


def send(piece, down, right):
    rows, cols = lax.axis_size("row"), lax.axis_size("col")
    if right == 0:
        return lax.ppermute(piece, "row", [(i, (i + down) % rows) for i in range(rows)])
    if down == 0:
        return lax.ppermute(piece, "col", [(i, (i + right) % cols) for i in range(cols)])
    route = [
        (r * cols + c, (r + down) % rows * cols + (c + right) % cols)
        for r in range(rows)
        for c in range(cols)
    ]
    return lax.ppermute(piece, ("row", "col"), route)


def to_window(part0, part1, part2, part3):
    return part3, send(part2, 0, -1), send(part1, -1, 0), send(part0, -1, -1)


def from_window(part0, part1, part2, part3):
    return send(part3, 1, 1), send(part2, 1, 0), send(part1, 0, 1), part0


def exchange(parts):
    return lax.all_to_all(parts, ("row", "col"), split_axis=0, concat_axis=0, tiled=True)


def swap(piece, bit):
    return lax.ppermute(piece, "col", [(i, i ^ bit) for i in range(lax.axis_size("col"))])


def pair_gather(block):
    cols = lax.axis_size("col")
    groups = [[g + i, g + i + 2] for g in range(0, cols, SPLIT) for i in range(2)]
    return lax.all_gather(block, "col", axis_index_groups=groups, axis=0, tiled=False)


def shards(
    image_map,
    qkv_weight,
    proj_weight,
    head_scale,
    bias_table,
    attn_gain,
    expert_ids,
    gate_prob,
    w_in,
    w_out,
    expert_gain,
    grad_out,
):
    width = image_map.shape[3]
    heads = head_scale.shape[0]
    row_count, col_count = lax.axis_size("row"), lax.axis_size("col")
    devices = row_count * col_count
    experts = devices // SPLIT
    cap = CELLS // experts
    slots = experts * cap
    tile = (WIN, WIN, width)
    quarter = (HALF, HALF, width)
    flat = (CELLS, width)
    parts = (devices, 2 * slots // devices, width)
    tile_img = image_map[0]
    img = tile_img.reshape(flat)
    grad = grad_out[0].reshape(flat)
    ids = expert_ids.reshape(WIN, WIN)
    gate = gate_prob.reshape(WIN, WIN)
    a_gain = attn_gain.reshape(1, width)
    e_gain = expert_gain.reshape(1, width)

    pieces = (tile_img[:HALF, :HALF], tile_img[:HALF, HALF:], tile_img[HALF:, :HALF])
    _, beside, below, corner = to_window(*pieces, None)
    first_w, second_w, _ = lax.optimization_barrier((w_in[0], w_out[0], pieces))
    near = pair_gather(jnp.concatenate([first_w, second_w], 0))
    edge = jnp.stack(
        [lax.axis_index("row") == row_count - 1, lax.axis_index("col") == col_count - 1]
    ).astype(jnp.int32)
    *attn_parts, qs, ku, vt, weights, aux, ho = call(
        attention_forward,
        [(quarter, BF16)] * 4
        + [((width, CELLS), BF16)] * 3
        + [
            ((heads, CELLS, CELLS), BF16),
            ((heads, 8, CELLS), F32),
            ((width, CELLS), BF16),
        ],
        [
            pltpu.VMEM((3 * width, CELLS), F32),
            pltpu.VMEM((TURNS, 8, WIN, 2 * CELLS), F32),
            pltpu.VMEM((CELLS, CELLS), F32),
            pltpu.VMEM((heads, 2 * CELLS), F32),
            pltpu.VMEM((heads, 2 * CELLS), F32),
        ],
        smem=2,
        total=9,
        gflop=8.0,
    )(edge, head_scale, tile_img, *in_vmem(beside, below, corner), qkv_weight, proj_weight, bias_table)
    att_parts = from_window(*attn_parts)
    ids, *_ = lax.optimization_barrier((ids, *attn_parts))
    place, grad_packed = call(
        lambda *refs: place_tokens(*refs, experts=experts, cap=cap),
        [((CELLS, slots), BF16), ((slots, width), BF16)],
        total=3,
        gflop=2.0,
    )(ids, gate, grad)
    packed, att = call(pack_residual, [(parts, BF16), (flat, BF16)], total=8)(
        *in_vmem(*att_parts), img, a_gain, place, grad_packed
    )
    near, _ = lax.optimization_barrier((near, packed))
    depth = w_in.shape[1]
    near = lax.optimization_barrier(
        (near[0, :depth], near[1, :depth], near[0, depth:], near[1, depth:])
    )
    far = [swap(block, 1) for block in near]
    sent = exchange(packed)
    rows, act, slope = call(
        expert_hidden,
        [(flat, BF16), ((SPLIT,) + flat, BF16), ((SPLIT,) + flat, BF16)],
        total=5,
        gflop=2.0,
    )(sent, *near[:2], *far[:2])
    next_rows = swap(rows, 2)
    d_expert, back = call(expert_rows, [(flat, BF16), (parts, BF16)], total=12, gflop=2.0)(
        sent, e_gain, act, slope, *near, *far
    )
    back, rows, next_rows = lax.optimization_barrier((back, rows, next_rows))
    back = exchange(back)
    across = swap(d_expert, 2)
    grads = (d_expert, swap(d_expert, 1), across, swap(across, 1))
    all_rows = (rows, swap(rows, 1), next_rows, swap(next_rows, 1))
    (both,) = call(
        expert_grads, [((w_in.shape[1], 2 * w_in.shape[2]), BF16)], total=10, gflop=7.0
    )(*all_rows, *grads, w_in[0], w_out[0])
    back, both = lax.optimization_barrier((back, both))
    both = lax.psum_scatter(both, "half", scatter_dimension=0, tiled=True).astype(F32)
    grad_w_in, grad_w_out = both[None, :, : w_in.shape[2]], both[None, :, w_in.shape[2] :]
    d_resid, *d_att = call(residual_grad, [(flat, F32)] + [(quarter, BF16)] * 4, total=5)(
        att, a_gain, place, grad, *in_vmem(back)
    )
    d_rolled = call(
        attention_backward,
        [(quarter, BF16)] * 4,
        [pltpu.VMEM((width, CELLS), F32), pltpu.VMEM((3 * width, CELLS), BF16)],
        smem=1,
        total=13,
        gflop=8.0,
    )(head_scale, d_att[3], *in_vmem(*to_window(*d_att)[1:]), qkv_weight, proj_weight, qs, ku, vt, weights, aux, ho)
    back, *_ = lax.optimization_barrier((back, *d_rolled))
    (block_out,) = call(finish_block, [(flat, BF16)], total=6)(
        att, img, a_gain, place, gate, back
    )
    top_left, top_right, bottom_left, bottom_right = from_window(*d_rolled)
    returned = jnp.concatenate(
        [
            jnp.concatenate([top_left, top_right], 1),
            jnp.concatenate([bottom_left, bottom_right], 1),
        ],
        0,
    )
    grad_map = (d_resid.reshape(tile) + returned.astype(F32)).astype(BF16)
    return (block_out.reshape(image_map.shape), grad_map[None], grad_w_in, grad_w_out)


def solution(mesh):
    tokens = P("half", "row", "col", None)
    in_specs = (
        tokens,
        P(),
        P(),
        P(),
        P(),
        P(),
        tokens,
        P("half", "row", "col"),
        P(("row", "col"), None, None),
        P(("row", "col"), None, None),
        P(),
        tokens,
    )
    out_specs = (
        tokens,
        tokens,
        P(("row", "col"), "half", None),
        P(("row", "col"), "half", None),
    )
    return jax.shard_map(shards, mesh=mesh, in_specs=in_specs, out_specs=out_specs, check_vma=False)
```

```python
import jax
import jax.numpy as jnp
from jax import lax
from jax.experimental import pallas as pl
from jax.experimental.pallas import tpu as pltpu
from jax.sharding import PartitionSpec as P

SPLIT = 4
WIN = 16
HALF = WIN // 2
CELLS = WIN * WIN
HEAD_W = 32
EPS = 1e-05
TURNS = 8
BF16 = jnp.bfloat16
F32 = jnp.float32
VMEM_BYTES = 24 * 1024 * 1024


def dotg(a, b, ca, cb):
    return lax.dot_general(a, b, (((ca,), (cb,)), ((), ())), preferred_element_type=F32)


def in_vmem(*arrays):
    return [pltpu.with_memory_space_constraint(a, pltpu.VMEM) for a in arrays]


def in_hbm(*arrays):
    return [pltpu.with_memory_space_constraint(a, pltpu.HBM) for a in arrays]


def call(body, outs, scratch=(), smem=0, total=0, gflop=1.0):
    in_specs = [pl.BlockSpec(memory_space=pltpu.SMEM)] * smem
    in_specs += [pl.BlockSpec(memory_space=pltpu.VMEM)] * (total - smem)
    return pl.pallas_call(
        body,
        out_shape=tuple(
            jax.ShapeDtypeStruct(s, d) if not kept else pltpu.HBM(s, d) for s, d, *kept in outs
        ),
        in_specs=in_specs,
        out_specs=tuple(pl.BlockSpec(memory_space=pltpu.VMEM) for _ in outs),
        scratch_shapes=list(scratch),
        compiler_params=pltpu.CompilerParams(vmem_limit_bytes=VMEM_BYTES),
        cost_estimate=pl.CostEstimate(
            flops=int(gflop * 1e9), bytes_accessed=1 << 20, transcendentals=0
        ),
    )


def assemble(parts):
    a, b, c, d = (part.astype(F32) for part in parts)
    whole = jnp.concatenate([jnp.concatenate([a, b], 1), jnp.concatenate([c, d], 1)], 0)
    return whole.reshape(CELLS, whole.shape[-1])


def store_parts(whole, refs):
    tile = whole.reshape(WIN, WIN, whole.shape[-1])
    for i, ref in enumerate(refs):
        r, c = HALF * (i // 2), HALF * (i % 2)
        ref[...] = tile[r : r + HALF, c : c + HALF].astype(BF16)


def spread_table(table, low, high):
    heads, entries = table.shape
    lanes = 2 * CELLS
    padded = jnp.concatenate([table[...], jnp.zeros((heads, 2 * lanes - entries), F32)], 1)
    row = lax.broadcasted_iota(jnp.int32, (heads, lanes), 1) >> 4
    low_rows = jnp.zeros((heads, lanes), F32)
    high_rows = jnp.zeros((heads, lanes), F32)
    for j in range(2 * WIN - 1):
        left = (WIN - 1) * j
        first = pltpu.roll(padded, (2 * lanes - left) % (2 * lanes), 1)[:, :lanes]
        other = pltpu.roll(padded, 2 * lanes - left - WIN, 1)[:, :lanes]
        low_rows = jnp.where(row == j, first, low_rows)
        high_rows = jnp.where(row == j, other, high_rows)
    low[...] = low_rows
    high[...] = high_rows


def attention_forward(
    edge, scale, img, beside, below, corner, wqkv, proj, table,
    out0, out1, out2, out3, qs, ku, vt, weights, aux, ho, prj, strips, mask, low, high,
):
    heads = scale.shape[0]
    width = heads * HEAD_W
    own = img[...].astype(F32)[HALF:, HALF:]
    x = assemble((own, beside[...], below[...], corner[...])).astype(BF16)
    prj[...] = dotg(wqkv[...], x, 0, 1)
    spread_table(table, low, high)
    key = lax.broadcasted_iota(jnp.int32, (CELLS, CELLS), 0)
    qry = lax.broadcasted_iota(jnp.int32, (CELLS, CELLS), 1)
    row_diff = jnp.where((key >> 7) != (qry >> 7), edge[0], 0)
    col_diff = jnp.where(((key >> 3) & 1) != ((qry >> 3) & 1), edge[1], 0)
    mask[...] = jnp.where(row_diff + col_diff > 0, -100.0, 0.0)
    lanes = 2 * CELLS
    sub = lax.broadcasted_iota(jnp.int32, (WIN, lanes), 0)
    lane = lax.broadcasted_iota(jnp.int32, (WIN, lanes), 1)
    from_low = (lane & (WIN - 1)) <= sub

    def head(h, turn):
        at = pl.multiple_of(h * HEAD_W, HEAD_W)
        q = prj[pl.ds(at, HEAD_W), :]
        k = prj[pl.ds(width + at, HEAD_W), :]
        v = prj[pl.ds(2 * width + at, HEAD_W), :].astype(BF16)
        q_sq = jnp.sum(q * q, 0, keepdims=True)
        k_sq = jnp.sum(k * k, 0, keepdims=True)
        q = (q * (lax.rsqrt(jnp.maximum(q_sq, 1.0)) * scale[h])).astype(BF16)
        k = (k * lax.rsqrt(jnp.maximum(k_sq, 1.0))).astype(BF16)
        qs[pl.ds(at, HEAD_W), :] = q
        ku[pl.ds(at, HEAD_W), :] = k
        vt[pl.ds(at, HEAD_W), :] = v
        scores = dotg(k, q, 0, 0)
        low_rows = jnp.broadcast_to(low[pl.ds(h, 1), :], (WIN, lanes))
        high_rows = jnp.broadcast_to(high[pl.ds(h, 1), :], (WIN, lanes))
        strip = jnp.where(
            from_low,
            pltpu.roll(low_rows, lanes - WIN + 1, 1, stride=1, stride_axis=0),
            pltpu.roll(high_rows, 1, 1, stride=1, stride_axis=0),
        )
        strips[turn, 0] = strip
        for m in range(1, 8):
            strips[turn, m] = pltpu.roll(strip, lanes - WIN * m, 1)
        total = jnp.zeros((WIN, CELLS), F32)
        for a in range(WIN):
            far, m = divmod((WIN - 1 - a), 8)
            rows = slice(WIN * a, WIN * (a + 1))
            bias = strips[turn, m, :, 128 * far : 128 * far + CELLS]
            w = jnp.exp(scores[rows] + bias + mask[rows, :])
            total = total + w
            weights[h, rows, :] = w.astype(BF16)
        inv = 1.0 / jnp.sum(total, 0, keepdims=True)
        aux[h, 0:1, :] = inv
        aux[h, 1:2, :] = q_sq
        aux[h, 2:3, :] = k_sq
        ho[pl.ds(at, HEAD_W), :] = (dotg(v, weights[h], 1, 0) * inv).astype(BF16)

    def heads_of(i, carry):
        for turn in range(TURNS):
            head(i * TURNS + turn, turn)
        return carry

    lax.fori_loop(0, heads // TURNS, heads_of, 0)
    store_parts(dotg(ho[...], proj[...], 0, 0), (out0, out1, out2, out3))


def attention_backward(
    scale, d0, d1, d2, d3, wqkv, proj, qs, ku, vt, weights, aux, ho,
    out0, out1, out2, out3, dho, dprj,
):
    heads = scale.shape[0]
    width = heads * HEAD_W
    d_out = assemble((d0[...], d1[...], d2[...], d3[...])).astype(BF16)
    dho[...] = dotg(proj[...], d_out, 1, 1)

    def unit_grad(d_unit, unit, sq):
        inner = jnp.sum(d_unit * unit, 0, keepdims=True)
        share = jnp.where(sq > 1.0, 1.0, jnp.where(sq == 1.0, 0.5, 0.0))
        return (d_unit - unit * (inner * share)) * lax.rsqrt(jnp.maximum(sq, 1.0))

    def head(h):
        at = pl.multiple_of(h * HEAD_W, HEAD_W)
        here = pl.ds(at, HEAD_W)
        q, k, v = qs[here, :], ku[here, :], vt[here, :]
        inv = aux[h, 0:1, :]
        d_ho = dho[here, :].astype(BF16).astype(F32)
        delta = jnp.sum(d_ho * ho[here, :].astype(F32), 0, keepdims=True) * inv
        d_ho = (d_ho * inv).astype(BF16)
        w = weights[h]
        d_w = dotg(v, d_ho, 0, 0)
        d_s = (w.astype(F32) * (d_w - delta)).astype(BF16)
        d_q = dotg(k, d_s, 1, 0) * scale[h]
        d_k = dotg(q, d_s, 1, 1)
        d_v = dotg(d_ho, w, 1, 1)
        q_unit = q.astype(F32) * (1.0 / scale[h])
        dprj[here, :] = unit_grad(d_q, q_unit, aux[h, 1:2, :]).astype(BF16)
        dprj[pl.ds(width + at, HEAD_W), :] = unit_grad(d_k, k.astype(F32), aux[h, 2:3, :]).astype(BF16)
        dprj[pl.ds(2 * width + at, HEAD_W), :] = d_v.astype(BF16)

    def heads_of(i, carry):
        for turn in range(TURNS):
            head(i * TURNS + turn)
        return carry

    lax.fori_loop(0, heads // TURNS, heads_of, 0)
    store_parts(dotg(dprj[...], wqkv[...], 0, 1), (out0, out1, out2, out3))


def normal(values):
    center = values - jnp.mean(values, -1, keepdims=True)
    rstd = lax.rsqrt(jnp.mean(center * center, -1, keepdims=True) + EPS)
    return center * rstd, rstd


def norm_grad(unit, rstd, d_unit):
    return rstd * (
        d_unit
        - jnp.mean(d_unit, -1, keepdims=True)
        - unit * jnp.mean(d_unit * unit, -1, keepdims=True)
    )


def column(field):
    row = lax.broadcasted_iota(jnp.int32, (CELLS, WIN), 0)
    col = lax.broadcasted_iota(jnp.int32, (CELLS, WIN), 1)
    pick = jnp.where((row >> 4) == col, 1.0, 0.0)
    rows = lax.dot_general(
        pick, field, (((1,), (0,)), ((), ())),
        preferred_element_type=F32, precision=lax.Precision.HIGHEST,
    )
    return jnp.sum(jnp.where((row & (WIN - 1)) == col, rows, 0.0), 1, keepdims=True)


def both_in(out, first, second):
    shape = (out.shape[0], out.shape[1] // 2, out.shape[2])
    out[...] = jnp.concatenate([first.reshape(shape), second.reshape(shape)], 1)


def one_of(both, which):
    count = both.shape[1] // 2
    part = both[:, which * count : (which + 1) * count, :]
    return part.reshape(part.shape[0] * count, part.shape[2])


def place_tokens(ids, gate, grad, place, packed, experts, cap):
    expert = column(ids[...].astype(F32)).astype(jnp.int32)
    matches = expert == lax.broadcasted_iota(jnp.int32, (CELLS, experts), 1)
    later = lax.broadcasted_iota(jnp.int32, (CELLS, CELLS), 0)
    sooner = lax.broadcasted_iota(jnp.int32, (CELLS, CELLS), 1)
    earlier = jnp.where(later > sooner, 1.0, 0.0).astype(BF16)
    before = dotg(earlier, jnp.where(matches, 1.0, 0.0).astype(BF16), 1, 0)
    slot = jnp.sum(jnp.where(matches, before, 0.0), 1, keepdims=True).astype(jnp.int32)
    target = jnp.where(slot < cap, expert * cap + slot, -1)
    slots = lax.broadcasted_iota(jnp.int32, (CELLS, experts * cap), 1)
    where_to = jnp.where(target == slots, 1.0, 0.0).astype(BF16)
    place[...] = where_to
    weighted = (grad[...].astype(F32) * column(gate[...])).astype(BF16)
    packed[...] = dotg(where_to, weighted, 0, 0).astype(BF16)


def pack_residual(att0, att1, att2, att3, img, gain, place, grad_packed, packed, att):
    attention = assemble((att0[...], att1[...], att2[...], att3[...]))
    att[...] = attention.astype(BF16)
    unit, _ = normal(attention)
    routed = (img[...].astype(F32) + unit * gain[...]).astype(BF16)
    both_in(packed, dotg(place[...], routed, 0, 0).astype(BF16), grad_packed[...])


def residual_grad(att, gain, place, grad, back, d_resid, d0, d1, d2, d3):
    unit, rstd = normal(att[...].astype(F32))
    total = grad[...].astype(F32) + dotg(place[...], one_of(back[...], 0), 1, 0)
    d_resid[...] = total
    store_parts(norm_grad(unit, rstd, total * gain[...]), (d0, d1, d2, d3))


def finish_block(att, img, gain, place, gate, back, out):
    unit, _ = normal(att[...].astype(F32))
    residual = img[...].astype(F32) + unit * gain[...]
    added = column(gate[...]) * dotg(place[...], one_of(back[...], 1), 1, 0)
    out[...] = (residual + added).astype(BF16)


def gelu_parts(hidden):
    cdf = 0.5 * (1.0 + lax.erf(hidden * 0.7071067811865476))
    pdf = jnp.exp(hidden * hidden * -0.5) * 0.3989422804014327
    return hidden * cdf, cdf + hidden * pdf


def expert_hidden(sent, block0, block1, block2, block3, rows, act, slope):
    here = one_of(sent[...], 0)
    rows[...] = here
    for s, ref in enumerate((block0, block1, block2, block3)):
        value, grad = gelu_parts(dotg(here, ref[...], 1, 0))
        act[s] = value.astype(BF16)
        slope[s] = grad.astype(BF16)


def expert_rows(sent, gain, act, slope, *refs):
    w_in, w_out = refs[0:2] + refs[4:6], refs[2:4] + refs[6:8]
    d_expert, own, back = refs[8:]
    flat = d_expert.shape
    grad = one_of(sent[...], 1)
    total = jnp.zeros(flat, F32)
    for s, v in enumerate(w_out):
        total = total + dotg(act[s], v[...], 1, 0).astype(BF16).astype(F32)
    unit, rstd = normal(total)
    mixed = (unit * gain[...]).astype(BF16)
    d_out = norm_grad(unit, rstd, grad.astype(F32) * gain[...]).astype(BF16)
    d_expert[...] = d_out
    own[0] = one_of(sent[...], 0)
    own[1] = d_out
    total = jnp.zeros(flat, F32)
    for s, (w, v) in enumerate(zip(w_in, w_out, strict=True)):
        d_hidden = (dotg(d_out, v[...], 1, 1) * slope[s].astype(F32)).astype(BF16)
        total = total + dotg(d_hidden, w[...], 1, 1).astype(BF16).astype(F32)
    both_in(back, total.astype(BF16), mixed)


def expert_grads(own, beside, rows2, grad2, rows3, grad3, w_in, w_out, both):
    d_in = jnp.zeros(w_in.shape, F32)
    d_out = jnp.zeros(w_out.shape, F32)
    pairs = [(ref.at[0], ref.at[1]) for ref in (own, beside)] + [(rows2, grad2), (rows3, grad3)]
    for part, grad in pairs:
        part = part[...]
        act, slope = gelu_parts(dotg(part, w_in[...], 1, 0))
        d_out = d_out + dotg(act.astype(BF16), grad[...], 0, 0)
        d_hidden = (dotg(grad[...], w_out[...], 1, 1) * slope).astype(BF16)
        d_in = d_in + dotg(part, d_hidden, 0, 0)
    both[:, : w_in.shape[1]] = d_in.astype(BF16)
    both[:, w_in.shape[1] :] = d_out.astype(BF16)


def send(piece, down, right):
    rows, cols = lax.axis_size("row"), lax.axis_size("col")
    if right == 0:
        return lax.ppermute(piece, "row", [(i, (i + down) % rows) for i in range(rows)])
    if down == 0:
        return lax.ppermute(piece, "col", [(i, (i + right) % cols) for i in range(cols)])
    route = [
        (r * cols + c, (r + down) % rows * cols + (c + right) % cols)
        for r in range(rows)
        for c in range(cols)
    ]
    return lax.ppermute(piece, ("row", "col"), route)


def to_window(part0, part1, part2, part3):
    return part3, send(part2, 0, -1), send(part1, -1, 0), send(part0, -1, -1)


def from_window(part0, part1, part2, part3):
    return send(part3, 1, 1), send(part2, 1, 0), send(part1, 0, 1), part0


def exchange(parts):
    return lax.all_to_all(parts, ("row", "col"), split_axis=0, concat_axis=0, tiled=True)


def swap(piece, bit):
    return lax.ppermute(piece, "col", [(i, i ^ bit) for i in range(lax.axis_size("col"))])


def pair_gather(block):
    cols = lax.axis_size("col")
    groups = [[g + i, g + i + 2] for g in range(0, cols, SPLIT) for i in range(2)]
    return lax.all_gather(block, "col", axis_index_groups=groups, axis=0, tiled=False)


def shards(
    image_map,
    qkv_weight,
    proj_weight,
    head_scale,
    bias_table,
    attn_gain,
    expert_ids,
    gate_prob,
    w_in,
    w_out,
    expert_gain,
    grad_out,
):
    width = image_map.shape[3]
    heads = head_scale.shape[0]
    row_count, col_count = lax.axis_size("row"), lax.axis_size("col")
    devices = row_count * col_count
    experts = devices // SPLIT
    cap = CELLS // experts
    slots = experts * cap
    tile = (WIN, WIN, width)
    quarter = (HALF, HALF, width)
    flat = (CELLS, width)
    parts = (devices, 2 * slots // devices, width)
    tile_img = image_map[0]
    img = tile_img.reshape(flat)
    grad = grad_out[0].reshape(flat)
    ids = expert_ids.reshape(WIN, WIN)
    gate = gate_prob.reshape(WIN, WIN)
    a_gain = attn_gain.reshape(1, width)
    e_gain = expert_gain.reshape(1, width)

    pieces = (tile_img[:HALF, :HALF], tile_img[:HALF, HALF:], tile_img[HALF:, :HALF])
    _, beside, below, corner = to_window(*pieces, None)
    first_w, second_w, _ = lax.optimization_barrier((w_in[0], w_out[0], pieces))
    near = pair_gather(jnp.concatenate([first_w, second_w], 0))
    edge = jnp.stack(
        [lax.axis_index("row") == row_count - 1, lax.axis_index("col") == col_count - 1]
    ).astype(jnp.int32)
    *attn_parts, qs, ku, vt, weights, aux, ho = call(
        attention_forward,
        [(quarter, BF16)] * 4
        + [((width, CELLS), BF16)] * 3
        + [
            ((heads, CELLS, CELLS), BF16, True),
            ((heads, 8, CELLS), F32),
            ((width, CELLS), BF16),
        ],
        [
            pltpu.VMEM((3 * width, CELLS), F32),
            pltpu.VMEM((TURNS, 8, WIN, 2 * CELLS), F32),
            pltpu.VMEM((CELLS, CELLS), F32),
            pltpu.VMEM((heads, 2 * CELLS), F32),
            pltpu.VMEM((heads, 2 * CELLS), F32),
        ],
        smem=2,
        total=9,
        gflop=8.0,
    )(edge, head_scale, tile_img, *in_vmem(beside, below, corner), qkv_weight, proj_weight, bias_table)
    att_parts = from_window(*attn_parts)
    ids, *_ = lax.optimization_barrier((ids, *attn_parts))
    place, grad_packed = call(
        lambda *refs: place_tokens(*refs, experts=experts, cap=cap),
        [((CELLS, slots), BF16), ((slots, width), BF16)],
        total=3,
        gflop=2.0,
    )(ids, gate, grad)
    packed, att = call(pack_residual, [(parts, BF16), (flat, BF16, True)], total=8)(
        *in_vmem(*att_parts), img, a_gain, place, grad_packed
    )
    near, _ = lax.optimization_barrier((near, packed))
    depth = w_in.shape[1]
    near = lax.optimization_barrier(
        (near[0, :depth], near[1, :depth], near[0, depth:], near[1, depth:])
    )
    far = [swap(block, 1) for block in near]
    sent = exchange(packed)
    rows, act, slope = call(
        expert_hidden,
        [(flat, BF16), ((SPLIT,) + flat, BF16), ((SPLIT,) + flat, BF16)],
        total=5,
        gflop=2.0,
    )(sent, *near[:2], *far[:2])
    next_rows = swap(rows, 2)
    d_expert, own, back = call(
        expert_rows, [(flat, BF16), ((2,) + flat, BF16), (parts, BF16)], total=12, gflop=2.0
    )(sent, e_gain, act, slope, *in_hbm(*near), *far)
    back, next_rows = lax.optimization_barrier((back, next_rows))
    back = exchange(back)
    across = swap(d_expert, 2)
    late, _ = lax.optimization_barrier((own, across))
    both_rows = (own, swap(late, 1), next_rows, across, swap(next_rows, 1), swap(across, 1))
    (both,) = call(
        expert_grads, [((w_in.shape[1], 2 * w_in.shape[2]), BF16)], total=8, gflop=5.0
    )(*in_hbm(*both_rows, w_in[0], w_out[0]))
    back, both = lax.optimization_barrier((back, both))
    both = lax.psum_scatter(both, "half", scatter_dimension=0, tiled=True)[None]
    grad_w_in = both[:, :, : w_in.shape[2]].astype(F32)
    grad_w_out = both[:, :, w_in.shape[2] :].astype(F32)
    d_resid, *d_att = call(residual_grad, [(flat, F32)] + [(quarter, BF16)] * 4, total=5)(
        *in_hbm(att), a_gain, *in_hbm(place), grad, *in_vmem(back)
    )
    d_rolled = call(
        attention_backward,
        [(quarter, BF16)] * 4,
        [pltpu.VMEM((width, CELLS), F32), pltpu.VMEM((3 * width, CELLS), BF16)],
        smem=1,
        total=13,
        gflop=8.0,
    )(head_scale, d_att[3], *in_vmem(*to_window(*d_att)[1:]), qkv_weight, proj_weight, qs, ku, vt, *in_hbm(weights), aux, ho)
    back, *_ = lax.optimization_barrier((back, *d_rolled))
    (block_out,) = call(finish_block, [(flat, BF16)], total=6)(
        *in_hbm(att), img, a_gain, place, gate, back
    )
    top_left, top_right, bottom_left, bottom_right = from_window(*d_rolled)
    returned = jnp.concatenate(
        [
            jnp.concatenate([top_left, top_right], 1),
            jnp.concatenate([bottom_left, bottom_right], 1),
        ],
        0,
    )
    grad_map = (d_resid.reshape(tile) + returned.astype(F32)).astype(BF16)
    return (block_out.reshape(image_map.shape), grad_map[None], grad_w_in, grad_w_out)


def solution(mesh):
    tokens = P("half", "row", "col", None)
    in_specs = (
        tokens,
        P(),
        P(),
        P(),
        P(),
        P(),
        tokens,
        P("half", "row", "col"),
        P(("row", "col"), None, None),
        P(("row", "col"), None, None),
        P(),
        tokens,
    )
    out_specs = (
        tokens,
        tokens,
        P(("row", "col"), "half", None),
        P(("row", "col"), "half", None),
    )
    return jax.shard_map(shards, mesh=mesh, in_specs=in_specs, out_specs=out_specs, check_vma=False)
```

```python
import jax
import jax.numpy as jnp
from jax import lax
from jax.experimental import pallas as pl
from jax.experimental.pallas import tpu as pltpu
from jax.sharding import PartitionSpec as P

SPLIT = 4
WIN = 16
HALF = WIN // 2
CELLS = WIN * WIN
HEAD_W = 32
EPS = 1e-05
TURNS = 16
BF16 = jnp.bfloat16
F32 = jnp.float32
VMEM_BYTES = 24 * 1024 * 1024


def dotg(a, b, ca, cb):
    return lax.dot_general(a, b, (((ca,), (cb,)), ((), ())), preferred_element_type=F32)


def in_vmem(*arrays):
    return [pltpu.with_memory_space_constraint(a, pltpu.VMEM) for a in arrays]


def in_hbm(*arrays):
    return [pltpu.with_memory_space_constraint(a, pltpu.HBM) for a in arrays]


def call(body, outs, scratch=(), smem=0, total=0, gflop=1.0):
    in_specs = [pl.BlockSpec(memory_space=pltpu.SMEM)] * smem
    in_specs += [pl.BlockSpec(memory_space=pltpu.VMEM)] * (total - smem)
    return pl.pallas_call(
        body,
        out_shape=tuple(
            jax.ShapeDtypeStruct(s, d) if not kept else pltpu.HBM(s, d) for s, d, *kept in outs
        ),
        in_specs=in_specs,
        out_specs=tuple(pl.BlockSpec(memory_space=pltpu.VMEM) for _ in outs),
        scratch_shapes=list(scratch),
        compiler_params=pltpu.CompilerParams(vmem_limit_bytes=VMEM_BYTES),
        cost_estimate=pl.CostEstimate(
            flops=int(gflop * 1e9), bytes_accessed=1 << 20, transcendentals=0
        ),
    )


def assemble(parts):
    a, b, c, d = (part.astype(F32) for part in parts)
    whole = jnp.concatenate([jnp.concatenate([a, b], 1), jnp.concatenate([c, d], 1)], 0)
    return whole.reshape(CELLS, whole.shape[-1])


def store_parts(whole, refs):
    tile = whole.reshape(WIN, WIN, whole.shape[-1])
    for i, ref in enumerate(refs):
        r, c = HALF * (i // 2), HALF * (i % 2)
        ref[...] = tile[r : r + HALF, c : c + HALF].astype(BF16)


def spread_table(table, low, high):
    heads, entries = table.shape
    lanes = 2 * CELLS
    padded = jnp.concatenate([table[...], jnp.zeros((heads, 2 * lanes - entries), F32)], 1)
    row = lax.broadcasted_iota(jnp.int32, (heads, lanes), 1) >> 4
    low_rows = jnp.zeros((heads, lanes), F32)
    high_rows = jnp.zeros((heads, lanes), F32)
    for j in range(2 * WIN - 1):
        left = (WIN - 1) * j
        first = pltpu.roll(padded, (2 * lanes - left) % (2 * lanes), 1)[:, :lanes]
        other = pltpu.roll(padded, 2 * lanes - left - WIN, 1)[:, :lanes]
        low_rows = jnp.where(row == j, first, low_rows)
        high_rows = jnp.where(row == j, other, high_rows)
    low[...] = low_rows
    high[...] = high_rows


def attention_forward(
    edge, scale, img, beside, below, corner, wqkv, proj, table,
    out0, out1, out2, out3, qs, ku, vt, weights, aux, ho, prj, strips, mask, low, high,
):
    heads = scale.shape[0]
    width = heads * HEAD_W
    own = img[...].astype(F32)[HALF:, HALF:]
    x = assemble((own, beside[...], below[...], corner[...])).astype(BF16)
    prj[...] = dotg(wqkv[...], x, 0, 1)
    spread_table(table, low, high)
    key = lax.broadcasted_iota(jnp.int32, (CELLS, CELLS), 0)
    qry = lax.broadcasted_iota(jnp.int32, (CELLS, CELLS), 1)
    row_diff = jnp.where((key >> 7) != (qry >> 7), edge[0], 0)
    col_diff = jnp.where(((key >> 3) & 1) != ((qry >> 3) & 1), edge[1], 0)
    mask[...] = jnp.where(row_diff + col_diff > 0, -100.0, 0.0)
    lanes = 2 * CELLS
    sub = lax.broadcasted_iota(jnp.int32, (WIN, lanes), 0)
    lane = lax.broadcasted_iota(jnp.int32, (WIN, lanes), 1)
    from_low = (lane & (WIN - 1)) <= sub

    def head(h, turn):
        at = pl.multiple_of(h * HEAD_W, HEAD_W)
        q = prj[pl.ds(at, HEAD_W), :]
        k = prj[pl.ds(width + at, HEAD_W), :]
        v = prj[pl.ds(2 * width + at, HEAD_W), :].astype(BF16)
        q_sq = jnp.sum(q * q, 0, keepdims=True)
        k_sq = jnp.sum(k * k, 0, keepdims=True)
        q = (q * (lax.rsqrt(jnp.maximum(q_sq, 1.0)) * scale[h])).astype(BF16)
        k = (k * lax.rsqrt(jnp.maximum(k_sq, 1.0))).astype(BF16)
        qs[pl.ds(at, HEAD_W), :] = q
        ku[pl.ds(at, HEAD_W), :] = k
        vt[pl.ds(at, HEAD_W), :] = v
        scores = dotg(k, q, 0, 0)
        low_rows = jnp.broadcast_to(low[pl.ds(h, 1), :], (WIN, lanes))
        high_rows = jnp.broadcast_to(high[pl.ds(h, 1), :], (WIN, lanes))
        strip = jnp.where(
            from_low,
            pltpu.roll(low_rows, lanes - WIN + 1, 1, stride=1, stride_axis=0),
            pltpu.roll(high_rows, 1, 1, stride=1, stride_axis=0),
        )
        strips[turn, 0] = strip
        for m in range(1, 8):
            strips[turn, m] = pltpu.roll(strip, lanes - WIN * m, 1)
        total = jnp.zeros((WIN, CELLS), F32)
        for a in range(WIN):
            far, m = divmod((WIN - 1 - a), 8)
            rows = slice(WIN * a, WIN * (a + 1))
            bias = strips[turn, m, :, 128 * far : 128 * far + CELLS]
            w = jnp.exp(scores[rows] + bias + mask[rows, :])
            total = total + w
            weights[h, rows, :] = w.astype(BF16)
        inv = 1.0 / jnp.sum(total, 0, keepdims=True)
        aux[h, 0:1, :] = inv
        aux[h, 1:2, :] = q_sq
        aux[h, 2:3, :] = k_sq
        ho[pl.ds(at, HEAD_W), :] = (dotg(v, weights[h], 1, 0) * inv).astype(BF16)

    def heads_of(i, carry):
        for turn in range(TURNS):
            head(i * TURNS + turn, turn)
        return carry

    lax.fori_loop(0, heads // TURNS, heads_of, 0)
    store_parts(dotg(ho[...], proj[...], 0, 0), (out0, out1, out2, out3))


def attention_backward(
    scale, d0, d1, d2, d3, wqkv, proj, qs, ku, vt, weights, aux, ho,
    out0, out1, out2, out3, dho, dprj,
):
    heads = scale.shape[0]
    width = heads * HEAD_W
    d_out = assemble((d0[...], d1[...], d2[...], d3[...])).astype(BF16)
    dho[...] = dotg(proj[...], d_out, 1, 1)

    def unit_grad(d_unit, unit, sq):
        inner = jnp.sum(d_unit * unit, 0, keepdims=True)
        share = jnp.where(sq > 1.0, 1.0, jnp.where(sq == 1.0, 0.5, 0.0))
        return (d_unit - unit * (inner * share)) * lax.rsqrt(jnp.maximum(sq, 1.0))

    def head(h):
        at = pl.multiple_of(h * HEAD_W, HEAD_W)
        here = pl.ds(at, HEAD_W)
        q, k, v = qs[here, :], ku[here, :], vt[here, :]
        inv = aux[h, 0:1, :]
        d_ho = dho[here, :].astype(BF16).astype(F32)
        delta = jnp.sum(d_ho * ho[here, :].astype(F32), 0, keepdims=True) * inv
        d_ho = (d_ho * inv).astype(BF16)
        w = weights[h]
        d_w = dotg(v, d_ho, 0, 0)
        d_s = (w.astype(F32) * (d_w - delta)).astype(BF16)
        d_q = dotg(k, d_s, 1, 0) * scale[h]
        d_k = dotg(q, d_s, 1, 1)
        d_v = dotg(d_ho, w, 1, 1)
        q_unit = q.astype(F32) * (1.0 / scale[h])
        dprj[here, :] = unit_grad(d_q, q_unit, aux[h, 1:2, :]).astype(BF16)
        dprj[pl.ds(width + at, HEAD_W), :] = unit_grad(d_k, k.astype(F32), aux[h, 2:3, :]).astype(BF16)
        dprj[pl.ds(2 * width + at, HEAD_W), :] = d_v.astype(BF16)

    def heads_of(i, carry):
        for turn in range(TURNS):
            head(i * TURNS + turn)
        return carry

    lax.fori_loop(0, heads // TURNS, heads_of, 0)
    store_parts(dotg(dprj[...], wqkv[...], 0, 1), (out0, out1, out2, out3))


def normal(values):
    center = values - jnp.mean(values, -1, keepdims=True)
    rstd = lax.rsqrt(jnp.mean(center * center, -1, keepdims=True) + EPS)
    return center * rstd, rstd


def norm_grad(unit, rstd, d_unit):
    return rstd * (
        d_unit
        - jnp.mean(d_unit, -1, keepdims=True)
        - unit * jnp.mean(d_unit * unit, -1, keepdims=True)
    )


def column(field):
    row = lax.broadcasted_iota(jnp.int32, (CELLS, WIN), 0)
    col = lax.broadcasted_iota(jnp.int32, (CELLS, WIN), 1)
    pick = jnp.where((row >> 4) == col, 1.0, 0.0)
    rows = lax.dot_general(
        pick, field, (((1,), (0,)), ((), ())),
        preferred_element_type=F32, precision=lax.Precision.HIGHEST,
    )
    return jnp.sum(jnp.where((row & (WIN - 1)) == col, rows, 0.0), 1, keepdims=True)


def both_in(out, first, second):
    shape = (out.shape[0], out.shape[1] // 2, out.shape[2])
    out[...] = jnp.concatenate([first.reshape(shape), second.reshape(shape)], 1)


def one_of(both, which):
    count = both.shape[1] // 2
    part = both[:, which * count : (which + 1) * count, :]
    return part.reshape(part.shape[0] * count, part.shape[2])


def place_tokens(ids, gate, grad, place, packed, experts, cap):
    expert = column(ids[...].astype(F32)).astype(jnp.int32)
    matches = expert == lax.broadcasted_iota(jnp.int32, (CELLS, experts), 1)
    later = lax.broadcasted_iota(jnp.int32, (CELLS, CELLS), 0)
    sooner = lax.broadcasted_iota(jnp.int32, (CELLS, CELLS), 1)
    earlier = jnp.where(later > sooner, 1.0, 0.0).astype(BF16)
    before = dotg(earlier, jnp.where(matches, 1.0, 0.0).astype(BF16), 1, 0)
    slot = jnp.sum(jnp.where(matches, before, 0.0), 1, keepdims=True).astype(jnp.int32)
    target = jnp.where(slot < cap, expert * cap + slot, -1)
    slots = lax.broadcasted_iota(jnp.int32, (CELLS, experts * cap), 1)
    where_to = jnp.where(target == slots, 1.0, 0.0).astype(BF16)
    place[...] = where_to
    weighted = (grad[...].astype(F32) * column(gate[...])).astype(BF16)
    packed[...] = dotg(where_to, weighted, 0, 0).astype(BF16)


def pack_residual(att0, att1, att2, att3, img, gain, place, grad_packed, packed, att):
    attention = assemble((att0[...], att1[...], att2[...], att3[...]))
    att[...] = attention.astype(BF16)
    unit, _ = normal(attention)
    routed = (img[...].astype(F32) + unit * gain[...]).astype(BF16)
    both_in(packed, dotg(place[...], routed, 0, 0).astype(BF16), grad_packed[...])


def residual_grad(att, gain, place, grad, back, d_resid, d0, d1, d2, d3):
    unit, rstd = normal(att[...].astype(F32))
    total = grad[...].astype(F32) + dotg(place[...], one_of(back[...], 0), 1, 0)
    d_resid[...] = total
    store_parts(norm_grad(unit, rstd, total * gain[...]), (d0, d1, d2, d3))


def finish_block(att, img, gain, place, gate, back, out):
    unit, _ = normal(att[...].astype(F32))
    residual = img[...].astype(F32) + unit * gain[...]
    added = column(gate[...]) * dotg(place[...], one_of(back[...], 1), 1, 0)
    out[...] = (residual + added).astype(BF16)


def gelu_parts(hidden):
    cdf = 0.5 * (1.0 + lax.erf(hidden * 0.7071067811865476))
    pdf = jnp.exp(hidden * hidden * -0.5) * 0.3989422804014327
    return hidden * cdf, cdf + hidden * pdf


def expert_hidden(sent, block0, block1, block2, block3, rows, act, slope):
    here = one_of(sent[...], 0)
    rows[...] = here
    for s, ref in enumerate((block0, block1, block2, block3)):
        value, grad = gelu_parts(dotg(here, ref[...], 1, 0))
        act[s] = value.astype(BF16)
        slope[s] = grad.astype(BF16)


def expert_rows(sent, gain, act, slope, *refs):
    w_in, w_out = refs[0:2] + refs[4:6], refs[2:4] + refs[6:8]
    d_expert, own, back = refs[8:]
    flat = d_expert.shape
    grad = one_of(sent[...], 1)
    total = jnp.zeros(flat, F32)
    for s, v in enumerate(w_out):
        total = total + dotg(act[s], v[...], 1, 0).astype(BF16).astype(F32)
    unit, rstd = normal(total)
    mixed = (unit * gain[...]).astype(BF16)
    d_out = norm_grad(unit, rstd, grad.astype(F32) * gain[...]).astype(BF16)
    d_expert[...] = d_out
    own[0] = one_of(sent[...], 0)
    own[1] = d_out
    total = jnp.zeros(flat, F32)
    for s, (w, v) in enumerate(zip(w_in, w_out, strict=True)):
        d_hidden = (dotg(d_out, v[...], 1, 1) * slope[s].astype(F32)).astype(BF16)
        total = total + dotg(d_hidden, w[...], 1, 1).astype(BF16).astype(F32)
    both_in(back, total.astype(BF16), mixed)


def expert_grads(own, beside, rows2, grad2, rows3, grad3, w_in, w_out, both):
    d_in = jnp.zeros(w_in.shape, F32)
    d_out = jnp.zeros(w_out.shape, F32)
    pairs = [(ref.at[0], ref.at[1]) for ref in (own, beside)] + [(rows2, grad2), (rows3, grad3)]
    for part, grad in pairs:
        part = part[...]
        act, slope = gelu_parts(dotg(part, w_in[...], 1, 0))
        d_out = d_out + dotg(act.astype(BF16), grad[...], 0, 0)
        d_hidden = (dotg(grad[...], w_out[...], 1, 1) * slope).astype(BF16)
        d_in = d_in + dotg(part, d_hidden, 0, 0)
    both[:, : w_in.shape[1]] = d_in.astype(BF16)
    both[:, w_in.shape[1] :] = d_out.astype(BF16)


def send(piece, down, right):
    rows, cols = lax.axis_size("row"), lax.axis_size("col")
    if right == 0:
        return lax.ppermute(piece, "row", [(i, (i + down) % rows) for i in range(rows)])
    if down == 0:
        return lax.ppermute(piece, "col", [(i, (i + right) % cols) for i in range(cols)])
    route = [
        (r * cols + c, (r + down) % rows * cols + (c + right) % cols)
        for r in range(rows)
        for c in range(cols)
    ]
    return lax.ppermute(piece, ("row", "col"), route)


def to_window(part0, part1, part2, part3):
    return part3, send(part2, 0, -1), send(part1, -1, 0), send(part0, -1, -1)


def from_window(part0, part1, part2, part3):
    return send(part3, 1, 1), send(part2, 1, 0), send(part1, 0, 1), part0


def exchange(parts):
    return lax.all_to_all(parts, ("row", "col"), split_axis=0, concat_axis=0, tiled=True)


def swap(piece, bit):
    return lax.ppermute(piece, "col", [(i, i ^ bit) for i in range(lax.axis_size("col"))])


def pair_gather(block):
    cols = lax.axis_size("col")
    groups = [[g + i, g + i + 2] for g in range(0, cols, SPLIT) for i in range(2)]
    return lax.all_gather(block, "col", axis_index_groups=groups, axis=0, tiled=False)


def shards(
    image_map,
    qkv_weight,
    proj_weight,
    head_scale,
    bias_table,
    attn_gain,
    expert_ids,
    gate_prob,
    w_in,
    w_out,
    expert_gain,
    grad_out,
):
    width = image_map.shape[3]
    heads = head_scale.shape[0]
    row_count, col_count = lax.axis_size("row"), lax.axis_size("col")
    devices = row_count * col_count
    experts = devices // SPLIT
    cap = CELLS // experts
    slots = experts * cap
    tile = (WIN, WIN, width)
    quarter = (HALF, HALF, width)
    flat = (CELLS, width)
    parts = (devices, 2 * slots // devices, width)
    tile_img = image_map[0]
    img = tile_img.reshape(flat)
    grad = grad_out[0].reshape(flat)
    ids = expert_ids.reshape(WIN, WIN)
    gate = gate_prob.reshape(WIN, WIN)
    a_gain = attn_gain.reshape(1, width)
    e_gain = expert_gain.reshape(1, width)

    pieces = (tile_img[:HALF, :HALF], tile_img[:HALF, HALF:], tile_img[HALF:, :HALF])
    _, beside, below, corner = to_window(*pieces, None)
    first_w, second_w, _ = lax.optimization_barrier((w_in[0], w_out[0], pieces))
    near = pair_gather(jnp.concatenate([first_w, second_w], 0))
    edge = jnp.stack(
        [lax.axis_index("row") == row_count - 1, lax.axis_index("col") == col_count - 1]
    ).astype(jnp.int32)
    *attn_parts, qs, ku, vt, weights, aux, ho = call(
        attention_forward,
        [(quarter, BF16)] * 4
        + [((width, CELLS), BF16)] * 3
        + [
            ((heads, CELLS, CELLS), BF16, True),
            ((heads, 8, CELLS), F32, True),
            ((width, CELLS), BF16),
        ],
        [
            pltpu.VMEM((3 * width, CELLS), F32),
            pltpu.VMEM((TURNS, 8, WIN, 2 * CELLS), F32),
            pltpu.VMEM((CELLS, CELLS), F32),
            pltpu.VMEM((heads, 2 * CELLS), F32),
            pltpu.VMEM((heads, 2 * CELLS), F32),
        ],
        smem=2,
        total=9,
        gflop=8.0,
    )(edge, head_scale, tile_img, *in_vmem(beside, below, corner), qkv_weight, proj_weight, bias_table)
    att_parts = from_window(*attn_parts)
    ids, *_ = lax.optimization_barrier((ids, *attn_parts))
    place, grad_packed = call(
        lambda *refs: place_tokens(*refs, experts=experts, cap=cap),
        [((CELLS, slots), BF16), ((slots, width), BF16)],
        total=3,
        gflop=2.0,
    )(ids, gate, grad)
    packed, att = call(pack_residual, [(parts, BF16), (flat, BF16, True)], total=8)(
        *in_vmem(*att_parts), img, a_gain, place, grad_packed
    )
    near, _ = lax.optimization_barrier((near, packed))
    depth = w_in.shape[1]
    near = lax.optimization_barrier(
        (near[0, :depth], near[1, :depth], near[0, depth:], near[1, depth:])
    )
    far = [swap(block, 1) for block in near]
    sent = exchange(packed)
    rows, act, slope = call(
        expert_hidden,
        [(flat, BF16), ((SPLIT,) + flat, BF16), ((SPLIT,) + flat, BF16)],
        total=5,
        gflop=2.0,
    )(sent, *near[:2], *far[:2])
    next_rows = swap(rows, 2)
    d_expert, own, back = call(
        expert_rows, [(flat, BF16), ((2,) + flat, BF16), (parts, BF16)], total=12, gflop=2.0
    )(sent, e_gain, act, slope, *in_hbm(*near), *far)
    back, next_rows = lax.optimization_barrier((back, next_rows))
    back = exchange(back)
    across = swap(d_expert, 2)
    late, _ = lax.optimization_barrier((own, across))
    both_rows = (own, swap(late, 1), next_rows, across, swap(next_rows, 1), swap(across, 1))
    (both,) = call(
        expert_grads, [((w_in.shape[1], 2 * w_in.shape[2]), BF16)], total=8, gflop=5.0
    )(*in_hbm(*both_rows, w_in[0], w_out[0]))
    back, both = lax.optimization_barrier((back, both))
    both = lax.psum_scatter(both, "half", scatter_dimension=0, tiled=True)[None]
    grad_w_in = both[:, :, : w_in.shape[2]].astype(F32)
    grad_w_out = both[:, :, w_in.shape[2] :].astype(F32)
    d_resid, *d_att = call(residual_grad, [(flat, F32)] + [(quarter, BF16)] * 4, total=5)(
        *in_hbm(att), a_gain, *in_hbm(place), grad, *in_vmem(back)
    )
    d_rolled = call(
        attention_backward,
        [(quarter, BF16)] * 4,
        [pltpu.VMEM((width, CELLS), F32), pltpu.VMEM((3 * width, CELLS), BF16)],
        smem=1,
        total=13,
        gflop=8.0,
    )(head_scale, d_att[3], *in_vmem(*to_window(*d_att)[1:]), qkv_weight, proj_weight, qs, ku, vt, *in_hbm(weights, aux), ho)
    back, *_ = lax.optimization_barrier((back, *d_rolled))
    (block_out,) = call(finish_block, [(flat, BF16)], total=6)(
        *in_hbm(att), img, a_gain, place, gate, back
    )
    top_left, top_right, bottom_left, bottom_right = from_window(*d_rolled)
    returned = jnp.concatenate(
        [
            jnp.concatenate([top_left, top_right], 1),
            jnp.concatenate([bottom_left, bottom_right], 1),
        ],
        0,
    )
    grad_map = (d_resid.reshape(tile) + returned.astype(F32)).astype(BF16)
    return (block_out.reshape(image_map.shape), grad_map[None], grad_w_in, grad_w_out)


def solution(mesh):
    tokens = P("half", "row", "col", None)
    in_specs = (
        tokens,
        P(),
        P(),
        P(),
        P(),
        P(),
        tokens,
        P("half", "row", "col"),
        P(("row", "col"), None, None),
        P(("row", "col"), None, None),
        P(),
        tokens,
    )
    out_specs = (
        tokens,
        tokens,
        P(("row", "col"), "half", None),
        P(("row", "col"), "half", None),
    )
    return jax.shard_map(shards, mesh=mesh, in_specs=in_specs, out_specs=out_specs, check_vma=False)
```
